32 devices in a mesh: tm: 2 (over core), height: 16 (over z, y, x).
Axes of the slice: x: 2, y: 2, z: 4, core: 2. Of those that a mesh axis runs over, the one named last changes fastest.
Arguments:
- queries: bfloat16 [8, 16, 32, 2560], P('tm', 'height'), may hold values from -8 to 8
- keys: bfloat16 [8, 16, 32, 2560], P('tm', 'height'), may hold values from -8 to 8
- values: bfloat16 [8, 16, 32, 2560], P('tm', 'height'), may hold values from -6 to 6
- window_mask: int32 [8, 16, 4, 27], P('tm', 'height'), may hold values from 0 to 1, as said below
- pos_t: int32 [8], P('tm'), may hold values from 0 to 127, as said below
- pos_h: int32 [16], P('height'), may hold values from 0 to 31, as said below
- pos_w: int32 [32], replicated, may hold values from 0 to 63, as said below
Outputs:
- attended: bfloat16 [8, 16, 32, 2560], P('tm', 'height')
The draws below stay inside these ranges and needn't reach their ends.
Inputs may be any that keep to these rules, and one draw needn't show every extreme that they name: `window_mask`: entry (dt+1)*9 + (dr+1)*3 + (db+1) refers to the tile offset by dt frames, dr rows and db tiles along the row; it is 0 wherever that tile lies outside the grid, and the centre entry 13 is always 1. `pos_t`: strictly increasing. `pos_h`: strictly increasing. `pos_w`: strictly increasing.
All inputs are finite; a program needn't handle non-finite values.
Results may differ from the reference program's by a relative error of at most 0.0044.
The reference program's roundings to bfloat16 on the way count: a program that leaves them out, or rounds other values in their place, can miss the bound.
Values may be sent and summed in bfloat16 or wider, within the bound.
A program may use at most 128 MiB of HBM per device.

```python
import math
import jax
import jax.numpy as jnp
from jax import lax

HEADS = 20
HEAD_DIM = 128
C = 2560
W = 32
TILE_W = 8
T_SIZE = 8
H = 16


def query_key_pair(key):
    base = jax.random.fold_in(key, 101)
    streams = jax.random.split(base, 2)
    full_shape = (T_SIZE, H, W, C)
    query_vals = 2.5 * jax.random.normal(streams[0], full_shape, jnp.float32)
    key_vals = jax.random.normal(streams[1], full_shape, jnp.float32)
    return (jnp.clip(query_vals, -8.0, 8.0), jnp.clip(key_vals, -8.0, 8.0))


def draw_queries(key, part):
    return query_key_pair(key)[0].astype(jnp.bfloat16)


def draw_keys(key, part):
    return query_key_pair(key)[1].astype(jnp.bfloat16)


def draw_window_mask(key, part):
    blocks = W // TILE_W
    frame_idx = jnp.arange(T_SIZE).reshape(T_SIZE, 1, 1, 1)
    row_idx = jnp.arange(H).reshape(1, H, 1, 1)
    block_idx = jnp.arange(blocks).reshape(1, 1, blocks, 1)
    offset = jnp.arange(27).reshape(1, 1, 1, 27)
    step_t = offset // 9 - 1
    step_h = offset // 3 % 3 - 1
    step_w = offset % 3 - 1
    inside = (frame_idx + step_t >= 0) & (frame_idx + step_t < T_SIZE) & (row_idx + step_h >= 0) & (row_idx + step_h < H) & (block_idx + step_w >= 0) & (block_idx + step_w < blocks)
    drawn = jax.random.randint(jax.random.fold_in(key, 7), (T_SIZE, H, blocks, 27), 0, 8)
    kept = drawn < 2 + 5 * frame_idx // T_SIZE
    return jnp.where(offset == 13, 1, jnp.where(kept & inside, 1, 0)).astype(jnp.int32)


def ordered_positions(key, length, salt):
    index_all = jnp.arange(length)
    extra = jax.random.randint(jax.random.fold_in(key, salt), (length,), 0, 2)
    positions = 2 * index_all + extra
    positions = jnp.where(index_all == 0, 0, jnp.where(index_all == length - 1, 2 * length - 1, positions))
    return positions.astype(jnp.int32)


def draw_pos_t(key, part):
    index_all = jnp.arange(T_SIZE)
    extra = jax.random.randint(jax.random.fold_in(key, 11), (T_SIZE,), 0, 16)
    return (16 * index_all + extra).astype(jnp.int32)


def draw_pos_h(key, part):
    return ordered_positions(key, H, 13)


def draw_pos_w(key, part):
    return ordered_positions(key, W, 17)


def block_levels(rng, extent, cuts, smallest, largest):
    def one(axis_at, parts):
        draws = jax.random.uniform(jax.random.fold_in(jax.random.fold_in(rng, 6), axis_at), (parts,), jnp.float32, smallest / len(cuts), largest / len(cuts))
        return jnp.repeat(jnp.exp(draws), extent[axis_at] // parts).reshape((-1,) + (1,) * (len(extent) - axis_at - 1))

    level = one(*cuts[0])
    for cut in cuts[1:]:
        level = level * one(*cut)
    return level


def scatter_about(key, dims, width, most, cuts=(), held_as=jnp.bfloat16):
    values = jax.random.normal(key, dims, jnp.float32) * width
    if len(cuts) > 0:
        values = block_levels(key, dims, cuts, -0.22, 0.18) * values
    return jnp.clip(values, min=-most, max=most).astype(held_as)


def setup_inputs(seed: int = 0) -> dict:
    key_of = jax.random.split(jax.random.key(seed), 8)
    return {
        "queries": draw_queries(jax.random.fold_in(key_of[7], 71), 0),
        "keys": draw_keys(jax.random.fold_in(key_of[7], 71), 0),
        "values": scatter_about(key_of[2], (T_SIZE, H, W, C), 1.0, 6.0, ((0, 2), (1, 16))),
        "window_mask": draw_window_mask(jax.random.fold_in(key_of[7], 71), 0),
        "pos_t": draw_pos_t(jax.random.fold_in(key_of[7], 71), 0),
        "pos_h": draw_pos_h(jax.random.fold_in(key_of[7], 71), 0),
        "pos_w": draw_pos_w(jax.random.fold_in(key_of[7], 71), 0),
    }


def rope_tables(pos_t, pos_h, pos_w, half_dim):
    pairs_hw = 2 * half_dim // 6
    pairs_time = half_dim - 2 * pairs_hw
    pair_index = jnp.arange(half_dim).astype(jnp.float32)
    freq_time = jnp.where(pair_index < pairs_time, jnp.power(10000.0, -pair_index / pairs_time), 0.0)
    in_rows = (pair_index >= pairs_time) & (pair_index < pairs_time + pairs_hw)
    freq_rows = jnp.where(in_rows, jnp.power(10000.0, -(pair_index - pairs_time) / pairs_hw), 0.0)
    freq_cols = jnp.where(pair_index >= pairs_time + pairs_hw, jnp.power(10000.0, -(pair_index - pairs_time - pairs_hw) / pairs_hw), 0.0)
    angles = pos_t.astype(jnp.float32)[:, None, None, None] * freq_time + pos_h.astype(jnp.float32)[None, :, None, None] * freq_rows + pos_w.astype(jnp.float32)[None, None, :, None] * freq_cols
    cos_tab = jnp.cos(angles)
    sine_tab = jnp.sin(angles)
    return (jnp.concatenate([cos_tab, cos_tab], -1), jnp.concatenate([-sine_tab, sine_tab], -1))

def rotate(tensor, cos_tab, sine_tab, head_count, head_dim):
    shaped = tensor.astype(jnp.float32).reshape(tensor.shape[:-1] + (head_count, head_dim))
    turned = shaped * cos_tab[..., None, :] + jnp.roll(shaped, head_dim // 2, axis=-1) * sine_tab[..., None, :]
    return turned.reshape(tensor.shape).astype(jnp.bfloat16)

def reference(queries, keys, values, window_mask, pos_t, pos_h, pos_w):
    head_count = HEADS
    head_dim = HEAD_DIM
    tile_len = TILE_W
    blocks = W // tile_len
    score_scale = 1.0 / math.sqrt(head_dim)
    cos_tab, sine_tab = rope_tables(pos_t, pos_h, pos_w, head_dim // 2)
    frame_list = jnp.arange(T_SIZE)

    def rotate_keys(frame_idx):
        return rotate(keys[frame_idx], cos_tab[frame_idx], sine_tab[frame_idx], head_count, head_dim)
    k_rot = lax.map(rotate_keys, frame_list)
    first_k = k_rot[0].reshape(H * W, head_count, head_dim).astype(jnp.float32)
    first_v = values[0].reshape(H * W, head_count, head_dim).astype(jnp.float32)
    padding = ((1, 1), (1, 1), (tile_len, tile_len), (0, 0))
    k_pad = jnp.pad(k_rot, padding)
    v_pad = jnp.pad(values, padding)

    def frame_out(frame_idx):
        q_rot = rotate(queries[frame_idx], cos_tab[frame_idx], sine_tab[frame_idx], head_count, head_dim)
        k_near = lax.dynamic_slice_in_dim(k_pad, frame_idx, 3, 0).reshape(3, H + 2, blocks + 2, tile_len, C)
        v_near = lax.dynamic_slice_in_dim(v_pad, frame_idx, 3, 0).reshape(3, H + 2, blocks + 2, tile_len, C)
        k_win = jnp.stack([k_near[step_t, step_h:step_h + H, step_w:step_w + blocks] for step_t in range(3) for step_h in range(3) for step_w in range(3)], axis=2)
        v_win = jnp.stack([v_near[step_t, step_h:step_h + H, step_w:step_w + blocks] for step_t in range(3) for step_h in range(3) for step_w in range(3)], axis=2)
        k_win = k_win.reshape(H, blocks, 27 * tile_len, head_count, head_dim).astype(jnp.float32)
        v_win = v_win.reshape(H, blocks, 27 * tile_len, head_count, head_dim).astype(jnp.float32)
        q_tiles = q_rot.reshape(H, blocks, tile_len, head_count, head_dim).astype(jnp.float32)
        s_near = jnp.einsum('abqhd,abkhd->abhqk', q_tiles, k_win) * score_scale
        allowed = jnp.repeat(window_mask[frame_idx] > 0, tile_len, axis=2)[:, :, None, None, :]
        q_flat = q_rot.reshape(H * W, head_count, head_dim).astype(jnp.float32)
        s_far = jnp.einsum('nhd,khd->hnk', q_flat, first_k) * score_scale
        s_far = s_far.reshape(head_count, H, blocks, tile_len, H * W).transpose(1, 2, 0, 3, 4)
        row_top = jnp.maximum(jnp.where(allowed, s_near, -1e+30).max(-1), s_far.max(-1))
        p_near = jnp.where(allowed, jnp.exp(s_near - row_top[..., None]), 0.0).astype(jnp.bfloat16)
        p_far = jnp.exp(s_far - row_top[..., None]).astype(jnp.bfloat16)
        row_total = p_near.astype(jnp.float32).sum(-1) + p_far.astype(jnp.float32).sum(-1)
        weighted = jnp.einsum('abhqk,abkhd->abqhd', p_near.astype(jnp.float32), v_win)
        weighted = weighted + jnp.einsum('abhqk,khd->abqhd', p_far.astype(jnp.float32), first_v)
        result = weighted / row_total.transpose(0, 1, 3, 2)[..., None]
        return result.reshape(H, W, C).astype(jnp.bfloat16)
    return lax.map(frame_out, frame_list)
```

```python
import functools
import math

import jax
import jax.numpy as jnp
import numpy as np
from jax import lax
from jax.experimental import pallas as pl
from jax.experimental.pallas import tpu as pltpu
from jax.sharding import PartitionSpec as P

HEADS = 20
HEAD_DIM = 128
TILE_W = 8
MESH = pl.DeviceIdType.MESH
NEAR = [(dc, dg) for dc in (-1, 0, 1) for dg in (-1, 0, 1) if (dc, dg) != (0, 0)]


def rope_tables(pos_t, pos_h, pos_w, half_dim):
    pairs_hw = 2 * half_dim // 6
    pairs_time = half_dim - 2 * pairs_hw
    pair_index = jnp.arange(half_dim).astype(jnp.float32)
    freq_time = jnp.where(
        pair_index < pairs_time, jnp.power(10000.0, -pair_index / pairs_time), 0.0
    )
    in_rows = (pair_index >= pairs_time) & (pair_index < pairs_time + pairs_hw)
    freq_rows = jnp.where(in_rows, jnp.power(10000.0, -(pair_index - pairs_time) / pairs_hw), 0.0)
    freq_cols = jnp.where(
        pair_index >= pairs_time + pairs_hw,
        jnp.power(10000.0, -(pair_index - pairs_time - pairs_hw) / pairs_hw),
        0.0,
    )
    angles = (
        pos_t.astype(jnp.float32)[:, None, None, None] * freq_time
        + pos_h.astype(jnp.float32)[None, :, None, None] * freq_rows
        + pos_w.astype(jnp.float32)[None, None, :, None] * freq_cols
    )
    cos_tab = jnp.cos(angles)
    sine_tab = jnp.sin(angles)
    return (jnp.concatenate([cos_tab, cos_tab], -1), jnp.concatenate([-sine_tab, sine_tab], -1))


def mask_selectors(group, width, lanes):
    blocks = width // TILE_W
    slot = lanes // blocks
    keys = 3 * (group + 2) * width
    own = (np.arange(width)[:, None] // TILE_W == np.arange(lanes)[None, :] // slot)
    key = np.arange(keys)
    step_t = key // ((group + 2) * width)
    key_row = key // width % (group + 2)
    key_block = key % width // TILE_W
    pick = np.zeros((group, lanes, keys), np.float32)
    for row in range(group):
        for block in range(blocks):
            step_h = key_row - row
            step_w = key_block - block + 1
            inside = (step_h >= 0) & (step_h < 3) & (step_w >= 0) & (step_w < 3)
            offset = step_t * 9 + step_h * 3 + step_w
            pick[row, (block * slot + offset)[inside], key[inside]] = 1.0
    return own.astype(np.float32), pick


def kernel(
    sizes, q_ref, k_ref, v_ref, cos_ref, sin_ref, mask_ref, own_ref, pick_ref, out_ref,
    rot, ext, first, held, masks, bias,
    a_send, a_recv, n_send, n_recv, f_send, f_recv, t_send, t_recv, o_send, o_recv, m_send, m_recv,
):
    group, groups, parts, frames, width, heads = sizes
    dim = HEAD_DIM
    tokens = group * width
    c = lax.axis_index("tm")
    at = lax.axis_index("height")
    g = at // group
    m = at % group

    def peer(step):
        return (m + step) % group

    def send_rows(j, step):
        to = peer(step)
        return pltpu.make_async_remote_copy(
            src_ref=rot.at[to * heads + j],
            dst_ref=ext.at[j, :, pl.ds(1, frames), m + 1],
            send_sem=a_send.at[j, step - 1],
            recv_sem=a_recv.at[j, m],
            device_id=(c, g * group + to),
            device_id_type=MESH,
        )

    def got_rows(j, step):
        come = peer(step)
        return pltpu.make_async_remote_copy(
            src_ref=rot.at[come * heads + j],
            dst_ref=ext.at[j, :, pl.ds(1, frames), come + 1],
            send_sem=a_send.at[j, step - 1],
            recv_sem=a_recv.at[j, come],
            device_id=(c, g * group + come),
            device_id_type=MESH,
        )

    def near_copy(j, n):
        dc, dg = NEAR[n]
        src_t = {-1: pl.ds(1, 1), 0: pl.ds(1, frames), 1: pl.ds(frames, 1)}[dc]
        dst_t = {-1: pl.ds(frames + 1, 1), 0: pl.ds(1, frames), 1: pl.ds(0, 1)}[dc]
        src_h = {-1: pl.ds(1, 1), 0: pl.ds(1, group), 1: pl.ds(group, 1)}[dg]
        dst_h = {-1: pl.ds(group + 1, 1), 0: pl.ds(1, group), 1: pl.ds(0, 1)}[dg]
        return pltpu.make_async_remote_copy(
            src_ref=ext.at[j, pl.ds(1, 2), src_t, src_h],
            dst_ref=ext.at[j, pl.ds(1, 2), dst_t, dst_h],
            send_sem=n_send.at[j, n],
            recv_sem=n_recv.at[j, n],
            device_id=(c + dc, at + dg * group),
            device_id_type=MESH,
        )

    def near_here(n, sign):
        dc, dg = sign * NEAR[n][0], sign * NEAR[n][1]
        ok = (c + dc >= 0) & (c + dc < parts)
        return ok & (g + dg >= 0) & (g + dg < groups)

    def first_copy(j, step):
        to = (g + step) % groups
        return pltpu.make_async_remote_copy(
            src_ref=ext.at[j, pl.ds(1, 2), 1, pl.ds(1, group)],
            dst_ref=first.at[j, :, pl.ds(g * group, group)],
            send_sem=f_send.at[j, step - 1],
            recv_sem=f_recv.at[j, g],
            device_id=(c, to * group + m),
            device_id_type=MESH,
        )

    def first_got(j, step):
        come = (g + step) % groups
        return pltpu.make_async_remote_copy(
            src_ref=ext.at[j, pl.ds(1, 2), 1, pl.ds(1, group)],
            dst_ref=first.at[j, :, pl.ds(come * group, group)],
            send_sem=f_send.at[j, step - 1],
            recv_sem=f_recv.at[j, come],
            device_id=(c, come * group + m),
            device_id_type=MESH,
        )

    def first_on(j, to):
        return pltpu.make_async_remote_copy(
            src_ref=first.at[j],
            dst_ref=first.at[j],
            send_sem=t_send.at[j, to - 1],
            recv_sem=t_recv.at[j],
            device_id=(to, at),
            device_id_type=MESH,
        )

    def columns(head):
        return pl.ds(pl.multiple_of(head * dim, dim), dim)

    def out_copy(j, step):
        to = peer(step)
        return pltpu.make_async_remote_copy(
            src_ref=held.at[j, to],
            dst_ref=out_ref.at[:, columns(m * heads + j)],
            send_sem=o_send.at[j, step - 1],
            recv_sem=o_recv.at[j, m],
            device_id=(c, g * group + to),
            device_id_type=MESH,
        )

    def out_got(j, step):
        come = peer(step)
        return pltpu.make_async_remote_copy(
            src_ref=held.at[j, come],
            dst_ref=out_ref.at[:, columns(come * heads + j)],
            send_sem=o_send.at[j, step - 1],
            recv_sem=o_recv.at[j, come],
            device_id=(c, g * group + come),
            device_id_type=MESH,
        )

    def mask_copy(step):
        return pltpu.make_async_remote_copy(
            src_ref=mask_ref,
            dst_ref=masks.at[m],
            send_sem=m_send.at[step - 1],
            recv_sem=m_recv.at[m],
            device_id=(c, g * group + peer(step)),
            device_id_type=MESH,
        )

    def mask_got(step):
        come = peer(step)
        return pltpu.make_async_remote_copy(
            src_ref=mask_ref,
            dst_ref=masks.at[come],
            send_sem=m_send.at[step - 1],
            recv_sem=m_recv.at[come],
            device_id=(c, g * group + come),
            device_id_type=MESH,
        )

    def turned(ref, head):
        x = ref[:, columns(head)].astype(jnp.float32)
        y = x * cos_ref[...] + pltpu.roll(x, dim // 2, 1) * sin_ref[...]
        return y.astype(jnp.bfloat16).reshape(frames, width, dim)

    def share(j):
        for step in range(1, group):
            head = peer(step) * heads + j
            rot[head, 0] = turned(q_ref, head)
            rot[head, 1] = turned(k_ref, head)
            rot[head, 2] = v_ref[:, columns(head)].reshape(frames, width, dim)
            send_rows(j, step).start()
        head = m * heads + j
        ext[j, 0, pl.ds(1, frames), m + 1] = turned(q_ref, head)
        ext[j, 1, pl.ds(1, frames), m + 1] = turned(k_ref, head)
        ext[j, 2, pl.ds(1, frames), m + 1] = v_ref[:, columns(head)].reshape(frames, width, dim)

    def clear(part):
        part[...] = jnp.zeros(part.shape, part.dtype)

    pl.when(c == 0)(lambda: clear(ext.at[:, pl.ds(1, 2), 0]))
    pl.when(c == parts - 1)(lambda: clear(ext.at[:, pl.ds(1, 2), frames + 1]))
    pl.when(g == 0)(lambda: clear(ext.at[:, pl.ds(1, 2), :, 0]))
    pl.when(g == groups - 1)(lambda: clear(ext.at[:, pl.ds(1, 2), :, group + 1]))

    barrier = pltpu.get_barrier_semaphore()
    for step in range(1, group):
        pl.semaphore_signal(barrier, inc=1, device_id=(c, g * group + peer(step)), device_id_type=MESH)
    for dt in range(parts):
        for dg in range(groups):
            if (dt, dg) != (0, 0):
                to = ((c + dt) % parts, (g + dg) % groups * group + m)
                pl.semaphore_signal(barrier, inc=1, device_id=to, device_id_type=MESH)
    pl.semaphore_wait(barrier, group - 1 + parts * groups - 1)

    for step in range(1, group):
        mask_copy(step).start()
    masks[m] = mask_ref[...]
    lax.fori_loop(0, min(2, heads), lambda j, x: (share(j), x)[1], 0)

    def spread_on(s):
        for step in range(1, group):
            got_rows(s, step).wait_recv()

        @pl.when(c == 0)
        def _():
            for step in range(1, groups):
                first_copy(s, step).start()

        for n in range(len(NEAR)):
            pl.when(near_here(n, 1))(lambda n=n: near_copy(s, n).start())

        pl.when(s + 2 < heads)(lambda: share(s + 2))

        @pl.when(c == 0)
        def _():
            first[s, :, pl.ds(g * group, group)] = ext[s, pl.ds(1, 2), 1, pl.ds(1, group)]

    def make_bias():
        for step in range(1, group):
            mask_got(step).wait_recv()
        for row in range(group):
            spread = jnp.concatenate(
                [jnp.broadcast_to(masks[row, f : f + 1, :], (width, masks.shape[2])) * own_ref[...] for f in range(frames)],
                axis=0,
            ).astype(jnp.bfloat16)
            allowed = jnp.dot(spread, pick_ref[row], preferred_element_type=jnp.float32)
            allowed = (allowed - 1.0) * 1e30
            bias[:, pl.ds(row * width, width)] = allowed.reshape(frames, width, allowed.shape[1])

    factor = math.log2(math.e) / math.sqrt(dim)

    def attend(j):
        @pl.when(c == 0)
        def _():
            for step in range(1, groups):
                first_got(j, step).wait_recv()
            for to in range(1, parts):
                first_on(j, to).start()

        pl.when(c > 0)(lambda: first_on(j, 1).wait_recv())
        for n in range(len(NEAR)):
            pl.when(near_here(n, -1))(lambda n=n: near_copy(j, n).wait_recv())

        far_k = first[j, 0].reshape(-1, dim)
        far_v = first[j, 1].reshape(-1, dim)
        far_v = jnp.concatenate([far_v, jnp.ones_like(far_v)], axis=1)
        last = (((1,), (1,)), ((), ()))
        for f in range(frames):
            q = ext[j, 0, 1 + f, pl.ds(1, group)].reshape(tokens, dim)
            near_k = ext[j, 1, pl.ds(f, 3)].reshape(-1, dim)
            near_v = ext[j, 2, pl.ds(f, 3)].reshape(-1, dim)
            near_v = jnp.concatenate([near_v, jnp.ones_like(near_v)], axis=1)
            s_near = lax.dot_general(q, near_k, last, preferred_element_type=jnp.float32) + bias[f]
            s_far = lax.dot_general(q, far_k, last, preferred_element_type=jnp.float32)
            top = jnp.maximum(
                jnp.max(s_near, axis=1, keepdims=True), jnp.max(s_far, axis=1, keepdims=True)
            )
            p_near = jnp.exp2((s_near - top) * factor).astype(jnp.bfloat16)
            p_far = jnp.exp2((s_far - top) * factor).astype(jnp.bfloat16)
            both = jnp.dot(p_near, near_v, preferred_element_type=jnp.float32)
            both = both + jnp.dot(p_far, far_v, preferred_element_type=jnp.float32)
            result = (both[:, :dim] / both[:, dim:]).astype(jnp.bfloat16)
            held[j, :, pl.ds(f * width, width)] = result.reshape(group, width, dim)
        for step in range(1, group):
            out_copy(j, step).start()
        out_ref[:, columns(m * heads + j)] = held[j, m]

    def turn(s, carry):
        pl.when(s < heads)(lambda: spread_on(s))
        pl.when(s == 0)(make_bias)
        pl.when(s > 0)(lambda: attend(s - 1))
        return carry

    lax.fori_loop(0, heads + 1, turn, 0)

    def finish(j, carry):
        for step in range(1, group):
            send_rows(j, step).wait_send()
            out_copy(j, step).wait_send()
            out_got(j, step).wait_recv()
        for n in range(len(NEAR)):
            pl.when(near_here(n, 1))(lambda n=n: near_copy(j, n).wait_send())

        @pl.when(c == 0)
        def _():
            for step in range(1, groups):
                first_copy(j, step).wait_send()
            for to in range(1, parts):
                first_on(j, to).wait_send()

        return carry

    lax.fori_loop(0, heads, finish, 0)
    for step in range(1, group):
        mask_copy(step).wait_send()


def per_device(parts, high, queries, keys, values, window_mask, pos_t, pos_h, pos_w):
    frames, row_count, width, channels = queries.shape
    assert row_count == 1
    dim = HEAD_DIM
    group = next(n for n in (4, 2, 1) if HEADS % n == 0 and high % n == 0)
    groups, heads = high // group, HEADS // group
    blocks = width // TILE_W
    lanes = 128
    cos_tab, sine_tab = rope_tables(pos_t, pos_h, pos_w, dim // 2)
    tokens = frames * width
    mask = jnp.pad((window_mask[:, 0] > 0).astype(jnp.float32), ((0, 0), (0, 0), (0, lanes // blocks - 27)))
    mask_rows = -(-frames // 8) * 8
    mask = jnp.pad(mask.reshape(frames, lanes), ((0, mask_rows - frames), (0, 0)))
    own, pick = mask_selectors(group, width, lanes)
    keys_near = pick.shape[2]
    sem = pltpu.SemaphoreType.DMA
    out = pl.pallas_call(
        functools.partial(kernel, (group, groups, parts, frames, width, heads)),
        out_shape=jax.ShapeDtypeStruct((tokens, channels), jnp.bfloat16),
        in_specs=[pl.BlockSpec(memory_space=pltpu.VMEM)] * 8,
        out_specs=pl.BlockSpec(memory_space=pltpu.VMEM),
        scratch_shapes=[
            pltpu.VMEM((HEADS, 3, frames, width, dim), jnp.bfloat16),
            pltpu.VMEM((heads, 3, frames + 2, group + 2, width, dim), jnp.bfloat16),
            pltpu.VMEM((heads, 2, high, width, dim), jnp.bfloat16),
            pltpu.VMEM((heads, group, tokens, dim), jnp.bfloat16),
            pltpu.VMEM((group, mask_rows, lanes), jnp.float32),
            pltpu.VMEM((frames, group * width, keys_near), jnp.float32),
            sem((heads, max(1, group - 1))),
            sem((heads, group)),
            sem((heads, len(NEAR))),
            sem((heads, len(NEAR))),
            sem((heads, max(1, groups - 1))),
            sem((heads, groups)),
            sem((heads, max(1, parts - 1))),
            sem((heads,)),
            sem((heads, max(1, group - 1))),
            sem((heads, group)),
            sem((max(1, group - 1),)),
            sem((group,)),
        ],
        compiler_params=pltpu.CompilerParams(
            collective_id=0, has_side_effects=True, vmem_limit_bytes=48 * 1024 * 1024
        ),
    )(
        queries.reshape(tokens, channels),
        keys.reshape(tokens, channels),
        values.reshape(tokens, channels),
        cos_tab.reshape(tokens, dim),
        sine_tab.reshape(tokens, dim),
        mask,
        jnp.asarray(own),
        jnp.asarray(pick, jnp.bfloat16),
    )
    return out.reshape(queries.shape)


def solution(mesh):
    return jax.shard_map(
        functools.partial(per_device, mesh.shape["tm"], mesh.shape["height"]),
        mesh=mesh,
        in_specs=(
            P("tm", "height", None, None),
            P("tm", "height", None, None),
            P("tm", "height", None, None),
            P("tm", "height", None, None),
            P("tm"),
            P("height"),
            P(),
        ),
        out_specs=P("tm", "height", None, None),
        check_vma=False,
    )
```

```python
import functools
import math

import jax
import jax.numpy as jnp
import numpy as np
from jax import lax
from jax.experimental import pallas as pl
from jax.experimental.pallas import tpu as pltpu
from jax.sharding import PartitionSpec as P

HEADS = 20
HEAD_DIM = 128
TILE_W = 8
MESH = pl.DeviceIdType.MESH
NEAR = [(dc, dg) for dc in (-1, 0, 1) for dg in (-1, 0, 1) if (dc, dg) != (0, 0)]


def frequencies(half_dim):
    pairs_hw = 2 * half_dim // 6
    pairs_time = half_dim - 2 * pairs_hw
    pair = np.arange(2 * half_dim) % half_dim
    count = np.where(pair < pairs_time, pairs_time, pairs_hw)
    first = np.where(pair < pairs_time, 0, np.where(pair < pairs_time + pairs_hw, pairs_time, pairs_time + pairs_hw))
    freq = 10000.0 ** (-(pair - first) / count)
    sign = np.where(np.arange(2 * half_dim) < half_dim, -1.0, 1.0)
    rows = [np.where(first == start, freq, 0.0) for start in (0, pairs_time, pairs_time + pairs_hw)]
    return np.stack(rows + [sign]).astype(np.float32)


def mask_selectors(group, width, lanes):
    blocks = width // TILE_W
    slot = lanes // blocks
    keys = 3 * (group + 2) * width
    own = (np.arange(width)[:, None] // TILE_W == np.arange(lanes)[None, :] // slot)
    key = np.arange(keys)
    step_t = key // ((group + 2) * width)
    key_row = key // width % (group + 2)
    key_block = key % width // TILE_W
    pick = np.zeros((group, lanes, keys), np.float32)
    for row in range(group):
        for block in range(blocks):
            step_h = key_row - row
            step_w = key_block - block + 1
            inside = (step_h >= 0) & (step_h < 3) & (step_w >= 0) & (step_w < 3)
            offset = step_t * 9 + step_h * 3 + step_w
            pick[row, (block * slot + offset)[inside], key[inside]] = 1.0
    return own.astype(np.float32), pick


def kernel(
    sizes, q_hbm, k_hbm, v_hbm, mask_hbm, pos_t_hbm, pos_h_ref, pos_w_hbm, const_hbm, pick_hbm, out_ref,
    q_ref, k_ref, v_ref, mask_in, pos_t_ref, pos_w_ref, const_ref, pick_ref,
    cos_ref, sin_ref, mask_pad, mask_ref, q_rot, rot, q_all, ext, first, held, masks, bias,
    load, q_send, q_recv, a_send, a_recv, n_send, n_recv, f_send, f_recv, t_send, t_recv, o_send, o_recv, m_send, m_recv,
):
    group, groups, parts, frames, width, heads = sizes
    dim = HEAD_DIM
    tokens = group * width
    c = lax.axis_index("tm")
    at = lax.axis_index("height")
    g = at // group
    m = at % group

    def peer(step):
        return (m + step) % group

    def row_copy(j, step, landing):
        other = peer(step)
        row = other if landing else m
        return pltpu.make_async_remote_copy(
            src_ref=rot.at[other * heads + j],
            dst_ref=ext.at[j, :, pl.ds(1, frames), row + 1],
            send_sem=a_send.at[j, step - 1],
            recv_sem=a_recv.at[j, row],
            device_id=(c, g * group + other),
            device_id_type=MESH,
        )

    def query_copy(j, step, landing):
        other = peer(step)
        row = other if landing else m
        return pltpu.make_async_remote_copy(
            src_ref=q_rot.at[other * heads + j],
            dst_ref=q_all.at[j, :, row],
            send_sem=q_send.at[j, step - 1],
            recv_sem=q_recv.at[j, row],
            device_id=(c, g * group + other),
            device_id_type=MESH,
        )

    def near_copy(j, n):
        dc, dg = NEAR[n]
        src_t = {-1: pl.ds(1, 1), 0: pl.ds(1, frames), 1: pl.ds(frames, 1)}[dc]
        dst_t = {-1: pl.ds(frames + 1, 1), 0: pl.ds(1, frames), 1: pl.ds(0, 1)}[dc]
        src_h = {-1: pl.ds(1, 1), 0: pl.ds(1, group), 1: pl.ds(group, 1)}[dg]
        dst_h = {-1: pl.ds(group + 1, 1), 0: pl.ds(1, group), 1: pl.ds(0, 1)}[dg]
        return pltpu.make_async_remote_copy(
            src_ref=ext.at[j, :, src_t, src_h],
            dst_ref=ext.at[j, :, dst_t, dst_h],
            send_sem=n_send.at[j, n],
            recv_sem=n_recv.at[j, n],
            device_id=(c + dc, at + dg * group),
            device_id_type=MESH,
        )

    def near_here(n, sign):
        dc, dg = sign * NEAR[n][0], sign * NEAR[n][1]
        ok = (c + dc >= 0) & (c + dc < parts)
        return ok & (g + dg >= 0) & (g + dg < groups)

    def first_copy(j, step):
        to = (g + step) % groups
        return pltpu.make_async_remote_copy(
            src_ref=ext.at[j, :, 1, pl.ds(1, group)],
            dst_ref=first.at[j, :, pl.ds(g * group, group)],
            send_sem=f_send.at[j, step - 1],
            recv_sem=f_recv.at[j, g],
            device_id=(c, to * group + m),
            device_id_type=MESH,
        )

    def first_got(j, step):
        come = (g + step) % groups
        return pltpu.make_async_remote_copy(
            src_ref=ext.at[j, :, 1, pl.ds(1, group)],
            dst_ref=first.at[j, :, pl.ds(come * group, group)],
            send_sem=f_send.at[j, step - 1],
            recv_sem=f_recv.at[j, come],
            device_id=(c, come * group + m),
            device_id_type=MESH,
        )

    def first_on(j, to):
        return pltpu.make_async_remote_copy(
            src_ref=first.at[j],
            dst_ref=first.at[j],
            send_sem=t_send.at[j, to - 1],
            recv_sem=t_recv.at[j],
            device_id=(to, at),
            device_id_type=MESH,
        )

    def columns(head):
        return pl.ds(pl.multiple_of(head * dim, dim), dim)

    def out_copy(j, step):
        to = peer(step)
        return pltpu.make_async_remote_copy(
            src_ref=held.at[j, to],
            dst_ref=out_ref.at[:, columns(m * heads + j)],
            send_sem=o_send.at[j, step - 1],
            recv_sem=o_recv.at[j, m],
            device_id=(c, g * group + to),
            device_id_type=MESH,
        )

    def out_got(j, step):
        come = peer(step)
        return pltpu.make_async_remote_copy(
            src_ref=held.at[j, come],
            dst_ref=out_ref.at[:, columns(come * heads + j)],
            send_sem=o_send.at[j, step - 1],
            recv_sem=o_recv.at[j, come],
            device_id=(c, g * group + come),
            device_id_type=MESH,
        )

    def mask_copy(step):
        return pltpu.make_async_remote_copy(
            src_ref=mask_ref,
            dst_ref=masks.at[m],
            send_sem=m_send.at[step - 1],
            recv_sem=m_recv.at[m],
            device_id=(c, g * group + peer(step)),
            device_id_type=MESH,
        )

    def mask_got(step):
        come = peer(step)
        return pltpu.make_async_remote_copy(
            src_ref=mask_ref,
            dst_ref=masks.at[come],
            send_sem=m_send.at[step - 1],
            recv_sem=m_recv.at[come],
            device_id=(c, g * group + come),
            device_id_type=MESH,
        )

    def turned(ref, head):
        x = ref[:, 0, :, columns(head)].astype(jnp.float32).reshape(frames * width, dim)
        y = x * cos_ref[...] + pltpu.roll(x, dim // 2, 1) * sin_ref[...]
        return y.astype(jnp.bfloat16).reshape(frames, width, dim)

    def make_rows(j):
        for step in range(1, group):
            head = peer(step) * heads + j
            rot[head, 0] = turned(k_ref, head)
            rot[head, 1] = v_ref[:, 0, :, columns(head)]
        head = m * heads + j
        ext[j, 0, pl.ds(1, frames), m + 1] = turned(k_ref, head)
        ext[j, 1, pl.ds(1, frames), m + 1] = v_ref[:, 0, :, columns(head)]

    def send_rows(j):
        for step in range(1, group):
            row_copy(j, step, False).start()

    def make_queries(j):
        for step in range(1, group):
            head = peer(step) * heads + j
            q_rot[head] = turned(q_ref, head)
        q_all[j, :, m] = turned(q_ref, m * heads + j)

    def send_queries(j):
        for step in range(1, group):
            query_copy(j, step, False).start()

    def clear(part):
        part[...] = jnp.zeros(part.shape, part.dtype)

    barrier = pltpu.get_barrier_semaphore()
    for step in range(1, group):
        pl.semaphore_signal(barrier, inc=1, device_id=(c, g * group + peer(step)), device_id_type=MESH)
    for dt in range(parts):
        for dg in range(groups):
            if (dt, dg) != (0, 0):
                to = ((c + dt) % parts, (g + dg) % groups * group + m)
                pl.semaphore_signal(barrier, inc=1, device_id=to, device_id_type=MESH)

    loads = [
        pltpu.make_async_copy(src, dst, load.at[n])
        for n, (src, dst) in enumerate(
            [
                (const_hbm, const_ref), (pos_t_hbm, pos_t_ref), (pos_w_hbm, pos_w_ref),
                (mask_hbm, mask_in), (k_hbm, k_ref), (v_hbm, v_ref), (q_hbm, q_ref), (pick_hbm, pick_ref),
            ]
        )
    ]
    for copy in loads:
        copy.start()

    pl.when(c == 0)(lambda: clear(ext.at[:, :, 0]))
    pl.when(c == parts - 1)(lambda: clear(ext.at[:, :, frames + 1]))
    pl.when(g == 0)(lambda: clear(ext.at[:, :, :, 0]))
    pl.when(g == groups - 1)(lambda: clear(ext.at[:, :, :, group + 1]))
    clear(mask_pad)

    for copy in loads[:4]:
        copy.wait()

    def column(ref, rows):
        row = ref[...].astype(jnp.float32)
        spread = jnp.broadcast_to(row, (rows, row.shape[1]))
        here = lax.broadcasted_iota(jnp.int32, spread.shape, 0) == lax.broadcasted_iota(jnp.int32, spread.shape, 1)
        return jnp.sum(jnp.where(here, spread, 0.0), axis=1, keepdims=True)

    freq_t = const_ref[width : width + 1, :]
    freq_h = const_ref[width + 1 : width + 2, :]
    freq_w = const_ref[width + 2 : width + 3, :]
    sign = const_ref[width + 3 : width + 4, :]
    pos_h = pos_h_ref[0].astype(jnp.float32)
    angle_hw = pos_h * freq_h + column(pos_w_ref, width) * freq_w
    angle_t = column(pos_t_ref, mask_ref.shape[0]) * freq_t
    for table, of, factor in ((cos_ref, jnp.cos, None), (sin_ref, jnp.sin, sign)):
        of_hw, of_t = of(angle_hw), of(angle_t)
        for f in range(frames):
            part = jnp.where(freq_t > 0, of_t[f : f + 1, :], of_hw)
            table[pl.ds(f * width, width), :] = part if factor is None else part * factor
    slot = mask_ref.shape[1] // mask_in.shape[2]
    for f in range(frames):
        mask_pad[f, pl.ds(0, mask_in.shape[2]), pl.ds(0, mask_in.shape[3])] = (mask_in[f, 0] > 0).astype(jnp.float32)
    clear(mask_ref)
    for f in range(frames):
        tile_rows = mask_pad[f]
        line = tile_rows[0:1, :]
        for b in range(1, mask_in.shape[2]):
            line = line + pltpu.roll(tile_rows, b * slot, 1)[b : b + 1, :]
        mask_ref[f : f + 1, :] = line
    masks[m] = mask_ref[...]

    loads[4].wait()
    loads[5].wait()
    make_rows(0)
    pl.semaphore_wait(barrier, group - 1 + parts * groups - 1)
    send_rows(0)
    if heads > 1:
        make_rows(1)
        send_rows(1)
    loads[6].wait()
    make_queries(0)
    send_queries(0)
    if heads > 2:
        make_rows(2)
        send_rows(2)
    for step in range(1, group):
        mask_copy(step).start()

    def spread_on(s):
        for step in range(1, group):
            row_copy(s, step, True).wait_recv()

        @pl.when(c == 0)
        def _():
            for step in range(1, groups):
                first_copy(s, step).start()

        for n in range(len(NEAR)):
            pl.when(near_here(n, 1))(lambda n=n: near_copy(s, n).start())

        def more_rows():
            make_rows(s + 3)
            send_rows(s + 3)

        def more_queries():
            make_queries(s + 1)
            send_queries(s + 1)

        pl.when(s + 3 < heads)(more_rows)
        pl.when(s + 1 < heads)(more_queries)

        @pl.when(c == 0)
        def _():
            first[s, :, pl.ds(g * group, group)] = ext[s, :, 1, pl.ds(1, group)]

    def make_bias():
        for step in range(1, group):
            mask_got(step).wait_recv()
        loads[7].wait()
        for row in range(group):
            spread = jnp.concatenate(
                [jnp.broadcast_to(masks[row, f : f + 1, :], (width, masks.shape[2])) * const_ref[0:width, :] for f in range(frames)],
                axis=0,
            ).astype(jnp.bfloat16)
            allowed = jnp.dot(spread, pick_ref[row], preferred_element_type=jnp.float32)
            allowed = (allowed - 1.0) * 1e30
            bias[:, pl.ds(row * width, width)] = allowed.reshape(frames, width, allowed.shape[1])

    factor = math.log2(math.e) / math.sqrt(dim)

    def attend(j):
        @pl.when(c == 0)
        def _():
            for step in range(1, groups):
                first_got(j, step).wait_recv()
            for to in range(1, parts):
                first_on(j, to).start()

        pl.when(c > 0)(lambda: first_on(j, 1).wait_recv())
        for n in range(len(NEAR)):
            pl.when(near_here(n, -1))(lambda n=n: near_copy(j, n).wait_recv())

        for step in range(1, group):
            query_copy(j, step, True).wait_recv()
        far_k = first[j, 0].reshape(-1, dim)
        far_v = first[j, 1].reshape(-1, dim)
        far_v = jnp.concatenate([far_v, jnp.ones_like(far_v)], axis=1)
        last = (((1,), (1,)), ((), ()))
        for f in range(frames):
            q = q_all[j, f].reshape(tokens, dim)
            near_k = ext[j, 0, pl.ds(f, 3)].reshape(-1, dim)
            near_v = ext[j, 1, pl.ds(f, 3)].reshape(-1, dim)
            near_v = jnp.concatenate([near_v, jnp.ones_like(near_v)], axis=1)
            s_near = lax.dot_general(q, near_k, last, preferred_element_type=jnp.float32) + bias[f]
            s_far = lax.dot_general(q, far_k, last, preferred_element_type=jnp.float32)
            top = jnp.maximum(
                jnp.max(s_near, axis=1, keepdims=True), jnp.max(s_far, axis=1, keepdims=True)
            )
            p_near = jnp.exp2((s_near - top) * factor).astype(jnp.bfloat16)
            p_far = jnp.exp2((s_far - top) * factor).astype(jnp.bfloat16)
            both = jnp.dot(p_near, near_v, preferred_element_type=jnp.float32)
            both = both + jnp.dot(p_far, far_v, preferred_element_type=jnp.float32)
            result = (both[:, :dim] / both[:, dim:]).astype(jnp.bfloat16)
            held[j, :, pl.ds(f * width, width)] = result.reshape(group, width, dim)
        for step in range(1, group):
            out_copy(j, step).start()
        out_ref[:, columns(m * heads + j)] = held[j, m]

    def turn(s, carry):
        pl.when(s < heads)(lambda: spread_on(s))
        pl.when(s == 0)(make_bias)
        pl.when(s > 0)(lambda: attend(s - 1))
        return carry

    lax.fori_loop(0, heads + 1, turn, 0)

    def finish(j, carry):
        for step in range(1, group):
            row_copy(j, step, False).wait_send()
            query_copy(j, step, False).wait_send()
            out_copy(j, step).wait_send()
            out_got(j, step).wait_recv()
        for n in range(len(NEAR)):
            pl.when(near_here(n, 1))(lambda n=n: near_copy(j, n).wait_send())

        @pl.when(c == 0)
        def _():
            for step in range(1, groups):
                first_copy(j, step).wait_send()
            for to in range(1, parts):
                first_on(j, to).wait_send()

        return carry

    lax.fori_loop(0, heads, finish, 0)
    for step in range(1, group):
        mask_copy(step).wait_send()


def per_device(parts, high, queries, keys, values, window_mask, pos_t, pos_h, pos_w):
    frames, row_count, width, channels = queries.shape
    assert row_count == 1
    dim = HEAD_DIM
    group = next(n for n in (4, 2, 1) if HEADS % n == 0 and high % n == 0)
    groups, heads = high // group, HEADS // group
    blocks = width // TILE_W
    lanes = 128
    tokens = frames * width
    mask_rows = -(-frames // 8) * 8
    own, pick = mask_selectors(group, width, lanes)
    const = np.concatenate([own, frequencies(dim // 2)], axis=0)
    const = np.pad(const, ((0, -len(const) % 8), (0, 0)))
    keys_near = pick.shape[2]
    sem = pltpu.SemaphoreType.DMA
    out = pl.pallas_call(
        functools.partial(kernel, (group, groups, parts, frames, width, heads)),
        out_shape=jax.ShapeDtypeStruct((tokens, channels), jnp.bfloat16),
        in_specs=[pl.BlockSpec(memory_space=pltpu.SMEM if n == 5 else pltpu.HBM) for n in range(9)],
        out_specs=pl.BlockSpec(memory_space=pltpu.VMEM),
        scratch_shapes=[
            pltpu.VMEM(queries.shape, jnp.bfloat16),
            pltpu.VMEM(queries.shape, jnp.bfloat16),
            pltpu.VMEM(queries.shape, jnp.bfloat16),
            pltpu.VMEM(window_mask.shape, jnp.int32),
            pltpu.VMEM((1, frames), jnp.int32),
            pltpu.VMEM((1, width), jnp.int32),
            pltpu.VMEM(const.shape, jnp.float32),
            pltpu.VMEM(pick.shape, jnp.bfloat16),
            pltpu.VMEM((tokens, dim), jnp.float32),
            pltpu.VMEM((tokens, dim), jnp.float32),
            pltpu.VMEM((frames, -(-blocks // 8) * 8, lanes), jnp.float32),
            pltpu.VMEM((mask_rows, lanes), jnp.float32),
            pltpu.VMEM((HEADS, frames, width, dim), jnp.bfloat16),
            pltpu.VMEM((HEADS, 2, frames, width, dim), jnp.bfloat16),
            pltpu.VMEM((heads, frames, group, width, dim), jnp.bfloat16),
            pltpu.VMEM((heads, 2, frames + 2, group + 2, width, dim), jnp.bfloat16),
            pltpu.VMEM((heads, 2, high, width, dim), jnp.bfloat16),
            pltpu.VMEM((heads, group, tokens, dim), jnp.bfloat16),
            pltpu.VMEM((group, mask_rows, lanes), jnp.float32),
            pltpu.VMEM((frames, group * width, keys_near), jnp.float32),
            sem((8,)),
            sem((heads, max(1, group - 1))),
            sem((heads, group)),
            sem((heads, max(1, group - 1))),
            sem((heads, group)),
            sem((heads, len(NEAR))),
            sem((heads, len(NEAR))),
            sem((heads, max(1, groups - 1))),
            sem((heads, groups)),
            sem((heads, max(1, parts - 1))),
            sem((heads,)),
            sem((heads, max(1, group - 1))),
            sem((heads, group)),
            sem((max(1, group - 1),)),
            sem((group,)),
        ],
        compiler_params=pltpu.CompilerParams(
            collective_id=0, has_side_effects=True, vmem_limit_bytes=62 * 1024 * 1024
        ),
    )(
        queries,
        keys,
        values,
        window_mask,
        pos_t.reshape(1, -1),
        pos_h,
        pos_w.reshape(1, -1),
        jnp.asarray(const),
        jnp.asarray(pick, jnp.bfloat16),
    )
    return out.reshape(queries.shape)


def solution(mesh):
    return jax.shard_map(
        functools.partial(per_device, mesh.shape["tm"], mesh.shape["height"]),
        mesh=mesh,
        in_specs=(
            P("tm", "height", None, None),
            P("tm", "height", None, None),
            P("tm", "height", None, None),
            P("tm", "height", None, None),
            P("tm"),
            P("height"),
            P(),
        ),
        out_specs=P("tm", "height", None, None),
        check_vma=False,
    )
```

```python
import functools
import math

import jax
import jax.numpy as jnp
import numpy as np
from jax import lax
from jax.experimental import pallas as pl
from jax.experimental.pallas import tpu as pltpu
from jax.sharding import PartitionSpec as P

HEADS = 20
HEAD_DIM = 128
TILE_W = 8
MESH = pl.DeviceIdType.MESH
NEAR = [(dc, dg) for dc in (-1, 0, 1) for dg in (-1, 0, 1) if (dc, dg) != (0, 0)]


def frequencies(half_dim):
    pairs_hw = 2 * half_dim // 6
    pairs_time = half_dim - 2 * pairs_hw
    pair = np.arange(2 * half_dim) % half_dim
    count = np.where(pair < pairs_time, pairs_time, pairs_hw)
    first = np.where(pair < pairs_time, 0, np.where(pair < pairs_time + pairs_hw, pairs_time, pairs_time + pairs_hw))
    freq = 10000.0 ** (-(pair - first) / count)
    sign = np.where(np.arange(2 * half_dim) < half_dim, -1.0, 1.0)
    rows = [np.where(first == start, freq, 0.0) for start in (0, pairs_time, pairs_time + pairs_hw)]
    return np.stack(rows + [sign]).astype(np.float32)


def mask_selectors(group, width, lanes):
    blocks = width // TILE_W
    slot = lanes // blocks
    keys = 3 * (group + 2) * width
    own = (np.arange(width)[:, None] // TILE_W == np.arange(lanes)[None, :] // slot)
    key = np.arange(keys)
    step_t = key // ((group + 2) * width)
    key_row = key // width % (group + 2)
    key_block = key % width // TILE_W
    pick = np.zeros((group, lanes, keys), np.float32)
    for row in range(group):
        for block in range(blocks):
            step_h = key_row - row
            step_w = key_block - block + 1
            inside = (step_h >= 0) & (step_h < 3) & (step_w >= 0) & (step_w < 3)
            offset = step_t * 9 + step_h * 3 + step_w
            pick[row, (block * slot + offset)[inside], key[inside]] = 1.0
    return own.astype(np.float32), pick


def kernel(
    sizes, q_hbm, k_hbm, v_hbm, mask_hbm, pos_t_hbm, pos_h_ref, pos_w_hbm, const_hbm, pick_hbm, out_ref,
    q_ref, k_ref, v_ref, mask_in, pos_t_ref, pos_w_ref, const_ref, pick_ref,
    cos_ref, sin_ref, mask_pad, mask_ref, q_rot, rot, q_all, ext, first, held, masks, bias,
    load, q_send, q_recv, a_send, a_recv, n_send, n_recv, f_send, f_recv, t_send, t_recv, o_send, o_recv, m_send, m_recv,
):
    group, groups, parts, frames, width, heads = sizes
    dim = HEAD_DIM
    tokens = group * width
    c = lax.axis_index("tm")
    at = lax.axis_index("height")
    g = at // group
    m = at % group

    def peer(step):
        return (m + step) % group

    def row_copy(j, step, landing):
        other = peer(step)
        row = other if landing else m
        return pltpu.make_async_remote_copy(
            src_ref=rot.at[other * heads + j],
            dst_ref=ext.at[j, :, pl.ds(1, frames), row + 1],
            send_sem=a_send.at[j, step - 1],
            recv_sem=a_recv.at[j, row],
            device_id=(c, g * group + other),
            device_id_type=MESH,
        )

    def query_copy(j, step, landing):
        other = peer(step)
        row = other if landing else m
        return pltpu.make_async_remote_copy(
            src_ref=q_rot.at[other * heads + j],
            dst_ref=q_all.at[j, :, row],
            send_sem=q_send.at[j, step - 1],
            recv_sem=q_recv.at[j, row],
            device_id=(c, g * group + other),
            device_id_type=MESH,
        )

    def near_copy(j, n):
        dc, dg = NEAR[n]
        src_t = {-1: pl.ds(1, 1), 0: pl.ds(1, frames), 1: pl.ds(frames, 1)}[dc]
        dst_t = {-1: pl.ds(frames + 1, 1), 0: pl.ds(1, frames), 1: pl.ds(0, 1)}[dc]
        src_h = {-1: pl.ds(1, 1), 0: pl.ds(1, group), 1: pl.ds(group, 1)}[dg]
        dst_h = {-1: pl.ds(group + 1, 1), 0: pl.ds(1, group), 1: pl.ds(0, 1)}[dg]
        return pltpu.make_async_remote_copy(
            src_ref=ext.at[j, :, src_t, src_h],
            dst_ref=ext.at[j, :, dst_t, dst_h],
            send_sem=n_send.at[j, n],
            recv_sem=n_recv.at[j, n],
            device_id=(c + dc, at + dg * group),
            device_id_type=MESH,
        )

    def near_here(n, sign):
        dc, dg = sign * NEAR[n][0], sign * NEAR[n][1]
        ok = (c + dc >= 0) & (c + dc < parts)
        return ok & (g + dg >= 0) & (g + dg < groups)

    def first_copy(j, step):
        to = (g + step) % groups
        return pltpu.make_async_remote_copy(
            src_ref=ext.at[j, :, 1, pl.ds(1, group)],
            dst_ref=first.at[j, :, pl.ds(g * group, group)],
            send_sem=f_send.at[j, step - 1],
            recv_sem=f_recv.at[j, g],
            device_id=(c, to * group + m),
            device_id_type=MESH,
        )

    def first_got(j, step):
        come = (g + step) % groups
        return pltpu.make_async_remote_copy(
            src_ref=ext.at[j, :, 1, pl.ds(1, group)],
            dst_ref=first.at[j, :, pl.ds(come * group, group)],
            send_sem=f_send.at[j, step - 1],
            recv_sem=f_recv.at[j, come],
            device_id=(c, come * group + m),
            device_id_type=MESH,
        )

    def first_on(j, to):
        return pltpu.make_async_remote_copy(
            src_ref=first.at[j],
            dst_ref=first.at[j],
            send_sem=t_send.at[j, to - 1],
            recv_sem=t_recv.at[j],
            device_id=(to, at),
            device_id_type=MESH,
        )

    def columns(head):
        return pl.ds(pl.multiple_of(head * dim, dim), dim)

    def out_copy(j, step):
        to = peer(step)
        return pltpu.make_async_remote_copy(
            src_ref=held.at[j, to],
            dst_ref=out_ref.at[:, columns(m * heads + j)],
            send_sem=o_send.at[j, step - 1],
            recv_sem=o_recv.at[j, m],
            device_id=(c, g * group + to),
            device_id_type=MESH,
        )

    def out_got(j, step):
        come = peer(step)
        return pltpu.make_async_remote_copy(
            src_ref=held.at[j, come],
            dst_ref=out_ref.at[:, columns(come * heads + j)],
            send_sem=o_send.at[j, step - 1],
            recv_sem=o_recv.at[j, come],
            device_id=(c, g * group + come),
            device_id_type=MESH,
        )

    def mask_copy(step):
        return pltpu.make_async_remote_copy(
            src_ref=mask_ref,
            dst_ref=masks.at[m],
            send_sem=m_send.at[step - 1],
            recv_sem=m_recv.at[m],
            device_id=(c, g * group + peer(step)),
            device_id_type=MESH,
        )

    def mask_got(step):
        come = peer(step)
        return pltpu.make_async_remote_copy(
            src_ref=mask_ref,
            dst_ref=masks.at[come],
            send_sem=m_send.at[step - 1],
            recv_sem=m_recv.at[come],
            device_id=(c, g * group + come),
            device_id_type=MESH,
        )

    def turned(ref, head):
        x = ref[:, 0, :, columns(head)].astype(jnp.float32).reshape(frames * width, dim)
        y = x * cos_ref[...] + pltpu.roll(x, dim // 2, 1) * sin_ref[...]
        return y.astype(jnp.bfloat16).reshape(frames, width, dim)

    def make_rows(j):
        for step in range(1, group):
            head = peer(step) * heads + j
            rot[head, 0] = turned(k_ref, head)
            rot[head, 1] = v_ref[:, 0, :, columns(head)]
        head = m * heads + j
        ext[j, 0, pl.ds(1, frames), m + 1] = turned(k_ref, head)
        ext[j, 1, pl.ds(1, frames), m + 1] = v_ref[:, 0, :, columns(head)]

    def send_rows(j):
        for step in range(1, group):
            row_copy(j, step, False).start()

    def make_queries(j):
        for step in range(1, group):
            head = peer(step) * heads + j
            q_rot[head] = turned(q_ref, head)
        q_all[j, :, m] = turned(q_ref, m * heads + j)

    def send_queries(j):
        for step in range(1, group):
            query_copy(j, step, False).start()

    def clear(part):
        part[...] = jnp.zeros(part.shape, part.dtype)

    barrier = pltpu.get_barrier_semaphore()
    for step in range(1, group):
        pl.semaphore_signal(barrier, inc=1, device_id=(c, g * group + peer(step)), device_id_type=MESH)
    for dt in range(parts):
        for dg in range(groups):
            if (dt, dg) != (0, 0):
                to = ((c + dt) % parts, (g + dg) % groups * group + m)
                pl.semaphore_signal(barrier, inc=1, device_id=to, device_id_type=MESH)

    loads = [
        pltpu.make_async_copy(src, dst, load.at[n])
        for n, (src, dst) in enumerate(
            [
                (const_hbm, const_ref), (pos_t_hbm, pos_t_ref), (pos_w_hbm, pos_w_ref),
                (mask_hbm, mask_in), (k_hbm, k_ref), (v_hbm, v_ref), (q_hbm, q_ref), (pick_hbm, pick_ref),
            ]
        )
    ]
    for copy in loads:
        copy.start()

    pl.when(c == 0)(lambda: clear(ext.at[:, :, 0]))
    pl.when(c == parts - 1)(lambda: clear(ext.at[:, :, frames + 1]))
    pl.when(g == 0)(lambda: clear(ext.at[:, :, :, 0]))
    pl.when(g == groups - 1)(lambda: clear(ext.at[:, :, :, group + 1]))
    clear(mask_pad)

    for copy in loads[:4]:
        copy.wait()

    def column(ref, rows):
        row = ref[...].astype(jnp.float32)
        spread = jnp.broadcast_to(row, (rows, row.shape[1]))
        here = lax.broadcasted_iota(jnp.int32, spread.shape, 0) == lax.broadcasted_iota(jnp.int32, spread.shape, 1)
        return jnp.sum(jnp.where(here, spread, 0.0), axis=1, keepdims=True)

    freq_t = const_ref[width : width + 1, :]
    freq_h = const_ref[width + 1 : width + 2, :]
    freq_w = const_ref[width + 2 : width + 3, :]
    sign = const_ref[width + 3 : width + 4, :]
    pos_h = pos_h_ref[0].astype(jnp.float32)
    angle_hw = pos_h * freq_h + column(pos_w_ref, width) * freq_w
    angle_t = column(pos_t_ref, mask_ref.shape[0]) * freq_t
    for table, of, factor in ((cos_ref, jnp.cos, None), (sin_ref, jnp.sin, sign)):
        of_hw, of_t = of(angle_hw), of(angle_t)
        for f in range(frames):
            part = jnp.where(freq_t > 0, of_t[f : f + 1, :], of_hw)
            table[pl.ds(f * width, width), :] = part if factor is None else part * factor
    slot = mask_ref.shape[1] // mask_in.shape[2]
    for f in range(frames):
        mask_pad[f, pl.ds(0, mask_in.shape[2]), pl.ds(0, mask_in.shape[3])] = (mask_in[f, 0] > 0).astype(jnp.float32)
    clear(mask_ref)
    for f in range(frames):
        tile_rows = mask_pad[f]
        line = tile_rows[0:1, :]
        for b in range(1, mask_in.shape[2]):
            line = line + pltpu.roll(tile_rows, b * slot, 1)[b : b + 1, :]
        mask_ref[f : f + 1, :] = line
    masks[m] = mask_ref[...]

    loads[4].wait()
    loads[5].wait()
    make_rows(0)
    pl.semaphore_wait(barrier, group - 1 + parts * groups - 1)
    send_rows(0)
    if heads > 1:
        make_rows(1)
        send_rows(1)
    if heads > 2:
        make_rows(2)
        send_rows(2)
    for step in range(1, group):
        mask_copy(step).start()

    def spread_on(s):
        for step in range(1, group):
            row_copy(s, step, True).wait_recv()

        @pl.when(c == 0)
        def _():
            for step in range(1, groups):
                first_copy(s, step).start()

        for n in range(len(NEAR)):
            pl.when(near_here(n, 1))(lambda n=n: near_copy(s, n).start())

        def more_rows():
            make_rows(s + 3)
            send_rows(s + 3)

        def more_queries():
            make_queries(s)
            send_queries(s)

        pl.when(s == 0)(loads[6].wait)
        more_queries()
        pl.when(s + 3 < heads)(more_rows)

        @pl.when(c == 0)
        def _():
            first[s, :, pl.ds(g * group, group)] = ext[s, :, 1, pl.ds(1, group)]

    def make_bias():
        for step in range(1, group):
            mask_got(step).wait_recv()
        loads[7].wait()
        for row in range(group):
            spread = jnp.concatenate(
                [jnp.broadcast_to(masks[row, f : f + 1, :], (width, masks.shape[2])) * const_ref[0:width, :] for f in range(frames)],
                axis=0,
            ).astype(jnp.bfloat16)
            allowed = jnp.dot(spread, pick_ref[row], preferred_element_type=jnp.float32)
            allowed = (allowed - 1.0) * 1e30
            bias[:, pl.ds(row * width, width)] = allowed.reshape(frames, width, allowed.shape[1])

    factor = math.log2(math.e) / math.sqrt(dim)

    def pass_on(j):
        for step in range(1, groups):
            first_got(j, step).wait_recv()
        for to in range(1, parts):
            first_on(j, to).start()

    def attend(j):
        pl.when(c > 0)(lambda: first_on(j, 1).wait_recv())
        for n in range(len(NEAR)):
            pl.when(near_here(n, -1))(lambda n=n: near_copy(j, n).wait_recv())

        for step in range(1, group):
            query_copy(j, step, True).wait_recv()
        far_k = first[j, 0].reshape(-1, dim)
        far_v = first[j, 1].reshape(-1, dim)
        far_v = jnp.concatenate([far_v, jnp.ones_like(far_v)], axis=1)
        last = (((1,), (1,)), ((), ()))
        s_all = lax.dot_general(
            q_all[j].reshape(frames * tokens, dim), far_k, last, preferred_element_type=jnp.float32
        )
        near, p_all = [], []
        for f in range(frames):
            q = q_all[j, f].reshape(tokens, dim)
            near_k = ext[j, 0, pl.ds(f, 3)].reshape(-1, dim)
            near_v = ext[j, 1, pl.ds(f, 3)].reshape(-1, dim)
            near_v = jnp.concatenate([near_v, jnp.ones_like(near_v)], axis=1)
            s_near = lax.dot_general(q, near_k, last, preferred_element_type=jnp.float32) + bias[f]
            s_far = s_all[f * tokens : (f + 1) * tokens]
            top = jnp.maximum(
                jnp.max(s_near, axis=1, keepdims=True), jnp.max(s_far, axis=1, keepdims=True)
            )
            p_near = jnp.exp2((s_near - top) * factor).astype(jnp.bfloat16)
            p_all.append(jnp.exp2((s_far - top) * factor).astype(jnp.bfloat16))
            near.append(jnp.dot(p_near, near_v, preferred_element_type=jnp.float32))
        far = jnp.dot(jnp.concatenate(p_all, axis=0), far_v, preferred_element_type=jnp.float32)
        for f in range(frames):
            both = near[f] + far[f * tokens : (f + 1) * tokens]
            result = (both[:, :dim] / both[:, dim:]).astype(jnp.bfloat16)
            held[j, :, pl.ds(f * width, width)] = result.reshape(group, width, dim)
        for step in range(1, group):
            out_copy(j, step).start()
        out_ref[:, columns(m * heads + j)] = held[j, m]

    def turn(s, carry):
        pl.when(s < heads)(lambda: spread_on(s))
        pl.when(s == 0)(make_bias)
        pl.when(s > 1)(lambda: attend(s - 2))
        pl.when((c == 0) & (s > 0) & (s <= heads))(lambda: pass_on(s - 1))
        return carry

    lax.fori_loop(0, heads + 2, turn, 0)

    def finish(j, carry):
        for step in range(1, group):
            row_copy(j, step, False).wait_send()
            query_copy(j, step, False).wait_send()
            out_copy(j, step).wait_send()
            out_got(j, step).wait_recv()
        for n in range(len(NEAR)):
            pl.when(near_here(n, 1))(lambda n=n: near_copy(j, n).wait_send())

        @pl.when(c == 0)
        def _():
            for step in range(1, groups):
                first_copy(j, step).wait_send()
            for to in range(1, parts):
                first_on(j, to).wait_send()

        return carry

    lax.fori_loop(0, heads, finish, 0)
    for step in range(1, group):
        mask_copy(step).wait_send()


def per_device(parts, high, queries, keys, values, window_mask, pos_t, pos_h, pos_w):
    frames, row_count, width, channels = queries.shape
    assert row_count == 1
    dim = HEAD_DIM
    group = next(n for n in (4, 2, 1) if HEADS % n == 0 and high % n == 0)
    groups, heads = high // group, HEADS // group
    blocks = width // TILE_W
    lanes = 128
    tokens = frames * width
    mask_rows = -(-frames // 8) * 8
    own, pick = mask_selectors(group, width, lanes)
    const = np.concatenate([own, frequencies(dim // 2)], axis=0)
    const = np.pad(const, ((0, -len(const) % 8), (0, 0)))
    keys_near = pick.shape[2]
    sem = pltpu.SemaphoreType.DMA
    in_hbm = functools.partial(pltpu.with_memory_space_constraint, memory_space=pltpu.HBM)
    out = pl.pallas_call(
        functools.partial(kernel, (group, groups, parts, frames, width, heads)),
        out_shape=jax.ShapeDtypeStruct((tokens, channels), jnp.bfloat16),
        in_specs=[pl.BlockSpec(memory_space=pltpu.SMEM if n == 5 else pltpu.HBM) for n in range(9)],
        out_specs=pl.BlockSpec(memory_space=pltpu.VMEM),
        scratch_shapes=[
            pltpu.VMEM(queries.shape, jnp.bfloat16),
            pltpu.VMEM(queries.shape, jnp.bfloat16),
            pltpu.VMEM(queries.shape, jnp.bfloat16),
            pltpu.VMEM(window_mask.shape, jnp.int32),
            pltpu.VMEM((1, frames), jnp.int32),
            pltpu.VMEM((1, width), jnp.int32),
            pltpu.VMEM(const.shape, jnp.float32),
            pltpu.VMEM(pick.shape, jnp.bfloat16),
            pltpu.VMEM((tokens, dim), jnp.float32),
            pltpu.VMEM((tokens, dim), jnp.float32),
            pltpu.VMEM((frames, -(-blocks // 8) * 8, lanes), jnp.float32),
            pltpu.VMEM((mask_rows, lanes), jnp.float32),
            pltpu.VMEM((HEADS, frames, width, dim), jnp.bfloat16),
            pltpu.VMEM((HEADS, 2, frames, width, dim), jnp.bfloat16),
            pltpu.VMEM((heads, frames, group, width, dim), jnp.bfloat16),
            pltpu.VMEM((heads, 2, frames + 2, group + 2, width, dim), jnp.bfloat16),
            pltpu.VMEM((heads, 2, high, width, dim), jnp.bfloat16),
            pltpu.VMEM((heads, group, tokens, dim), jnp.bfloat16),
            pltpu.VMEM((group, mask_rows, lanes), jnp.float32),
            pltpu.VMEM((frames, group * width, keys_near), jnp.float32),
            sem((8,)),
            sem((heads, max(1, group - 1))),
            sem((heads, group)),
            sem((heads, max(1, group - 1))),
            sem((heads, group)),
            sem((heads, len(NEAR))),
            sem((heads, len(NEAR))),
            sem((heads, max(1, groups - 1))),
            sem((heads, groups)),
            sem((heads, max(1, parts - 1))),
            sem((heads,)),
            sem((heads, max(1, group - 1))),
            sem((heads, group)),
            sem((max(1, group - 1),)),
            sem((group,)),
        ],
        compiler_params=pltpu.CompilerParams(
            collective_id=0, has_side_effects=True, vmem_limit_bytes=48 * 1024 * 1024
        ),
    )(
        *(in_hbm(x) for x in (queries, keys, values, window_mask)),
        in_hbm(pos_t.reshape(1, -1)),
        pos_h,
        in_hbm(pos_w.reshape(1, -1)),
        in_hbm(jnp.asarray(const)),
        in_hbm(jnp.asarray(pick, jnp.bfloat16)),
    )
    return out.reshape(queries.shape)


def solution(mesh):
    return jax.shard_map(
        functools.partial(per_device, mesh.shape["tm"], mesh.shape["height"]),
        mesh=mesh,
        in_specs=(
            P("tm", "height", None, None),
            P("tm", "height", None, None),
            P("tm", "height", None, None),
            P("tm", "height", None, None),
            P("tm"),
            P("height"),
            P(),
        ),
        out_specs=P("tm", "height", None, None),
        check_vma=False,
    )
```

```python
import functools
import math

import jax
import jax.numpy as jnp
import numpy as np
from jax import lax
from jax.experimental import pallas as pl
from jax.experimental.pallas import tpu as pltpu
from jax.sharding import PartitionSpec as P

HEADS = 20
HEAD_DIM = 128
TILE_W = 8
MESH = pl.DeviceIdType.MESH
NEAR = [(dc, dg) for dc in (-1, 0, 1) for dg in (-1, 0, 1) if (dc, dg) != (0, 0)]
ROWS = [n for n, (dc, dg) in enumerate(NEAR) if dc == 0]
CORNERS = [n for n, (dc, dg) in enumerate(NEAR) if dc != 0 and dg != 0]


def frequencies(half_dim):
    pairs_hw = 2 * half_dim // 6
    pairs_time = half_dim - 2 * pairs_hw
    pair = np.arange(2 * half_dim) % half_dim
    count = np.where(pair < pairs_time, pairs_time, pairs_hw)
    first = np.where(pair < pairs_time, 0, np.where(pair < pairs_time + pairs_hw, pairs_time, pairs_time + pairs_hw))
    freq = 10000.0 ** (-(pair - first) / count)
    sign = np.where(np.arange(2 * half_dim) < half_dim, -1.0, 1.0)
    rows = [np.where(first == start, freq, 0.0) for start in (0, pairs_time, pairs_time + pairs_hw)]
    return np.stack(rows + [sign]).astype(np.float32)


def mask_selectors(group, width, lanes):
    blocks = width // TILE_W
    slot = lanes // blocks
    keys = 3 * (group + 2) * width
    own = (np.arange(width)[:, None] // TILE_W == np.arange(lanes)[None, :] // slot)
    key = np.arange(keys)
    step_t = key // ((group + 2) * width)
    key_row = key // width % (group + 2)
    key_block = key % width // TILE_W
    pick = np.zeros((group, lanes, keys), np.float32)
    for row in range(group):
        for block in range(blocks):
            step_h = key_row - row
            step_w = key_block - block + 1
            inside = (step_h >= 0) & (step_h < 3) & (step_w >= 0) & (step_w < 3)
            offset = step_t * 9 + step_h * 3 + step_w
            pick[row, (block * slot + offset)[inside], key[inside]] = 1.0
    return own.astype(np.float32), pick


def kernel(
    sizes, q_hbm, k_hbm, v_hbm, mask_hbm, pos_t_hbm, pos_h_ref, pos_w_hbm, const_hbm, pick_hbm, out_ref,
    q_ref, k_ref, v_ref, mask_in, pos_t_ref, pos_w_ref, const_ref, pick_ref,
    cos_ref, sin_ref, mask_pad, mask_ref, q_rot, rot, q_all, ext, first, held, masks, bias,
    load, kv_load, q_send, q_recv, a_send, a_recv, n_send, n_recv, f_send, f_recv, r_send, r_recv, t_send, t_recv, o_send, o_recv, m_send, m_recv,
):
    group, groups, parts, frames, width, heads = sizes
    dim = HEAD_DIM
    tokens = group * width
    c = lax.axis_index("tm")
    at = lax.axis_index("height")
    g = at // group
    m = at % group

    def peer(step):
        return (m + step) % group

    def row_copy(j, step, landing):
        other = peer(step)
        row = other if landing else m
        return pltpu.make_async_remote_copy(
            src_ref=rot.at[other * heads + j],
            dst_ref=ext.at[j, :, pl.ds(1, frames), row + 1],
            send_sem=a_send.at[j, step - 1],
            recv_sem=a_recv.at[j, row],
            device_id=(c, g * group + other),
            device_id_type=MESH,
        )

    def query_copy(j, step, landing):
        other = peer(step)
        row = other if landing else m
        return pltpu.make_async_remote_copy(
            src_ref=q_rot.at[other * heads + j],
            dst_ref=q_all.at[j, :, row],
            send_sem=q_send.at[j, step - 1],
            recv_sem=q_recv.at[j, row],
            device_id=(c, g * group + other),
            device_id_type=MESH,
        )

    def near_copy(j, n):
        dc, dg = NEAR[n]
        src_t = {-1: pl.ds(1, 1), 0: pl.ds(1, frames), 1: pl.ds(frames, 1)}[dc]
        dst_t = {-1: pl.ds(frames + 1, 1), 0: pl.ds(1, frames), 1: pl.ds(0, 1)}[dc]
        if n in CORNERS:
            src_h = dst_h = pl.ds(0 if dg < 0 else group + 1, 1)
        else:
            src_h = {-1: pl.ds(1, 1), 0: pl.ds(1, group), 1: pl.ds(group, 1)}[dg]
            dst_h = {-1: pl.ds(group + 1, 1), 0: pl.ds(1, group), 1: pl.ds(0, 1)}[dg]
        return pltpu.make_async_remote_copy(
            src_ref=ext.at[j, :, src_t, src_h],
            dst_ref=ext.at[j, :, dst_t, dst_h],
            send_sem=n_send.at[j, n],
            recv_sem=n_recv.at[j, n],
            device_id=(c + dc, at if n in CORNERS else at + dg * group),
            device_id_type=MESH,
        )

    def near_here(n, sign):
        dc, dg = sign * NEAR[n][0], NEAR[n][1] if n in CORNERS else sign * NEAR[n][1]
        ok = (c + dc >= 0) & (c + dc < parts)
        return ok & (g + dg >= 0) & (g + dg < groups)

    def first_copy(j, to, owner, n):
        return pltpu.make_async_remote_copy(
            src_ref=ext.at[j, :, 1, pl.ds(1, group)],
            dst_ref=first.at[j, :, pl.ds(owner * group, group)],
            send_sem=f_send.at[j, n],
            recv_sem=f_recv.at[j, owner],
            device_id=(c, to * group + m),
            device_id_type=MESH,
        )

    half = groups // 2 if groups % 2 == 0 and groups > 2 else groups
    side = g // half
    gate = (g == half) | (g == half - 1)

    def beside(step):
        return side * half + (g % half + step) % half

    def first_targets():
        own_half = [beside(step) for step in range(1, half)]
        return own_half + ([half - side] if half < groups else [])

    def hand_copy(j, step):
        rows = pl.ds((1 - side) * half * group, half * group)
        return pltpu.make_async_remote_copy(
            src_ref=first.at[j, :, rows],
            dst_ref=first.at[j, :, rows],
            send_sem=r_send.at[j, step - 1],
            recv_sem=r_recv.at[j],
            device_id=(c, beside(step) * group + m),
            device_id_type=MESH,
        )

    def hand_on(j):
        for n in range(half):
            first_copy(j, (1 - side) * half + n, (1 - side) * half + n, 0).wait_recv()
        for step in range(1, half):
            hand_copy(j, step).start()

    def first_on(j, to):
        return pltpu.make_async_remote_copy(
            src_ref=first.at[j],
            dst_ref=first.at[j],
            send_sem=t_send.at[j, to - 1],
            recv_sem=t_recv.at[j],
            device_id=(to, at),
            device_id_type=MESH,
        )

    def columns(head):
        return pl.ds(pl.multiple_of(head * dim, dim), dim)

    def out_copy(j, step):
        to = peer(step)
        return pltpu.make_async_remote_copy(
            src_ref=held.at[j, to],
            dst_ref=out_ref.at[:, columns(m * heads + j)],
            send_sem=o_send.at[j, step - 1],
            recv_sem=o_recv.at[j, m],
            device_id=(c, g * group + to),
            device_id_type=MESH,
        )

    def out_got(j, step):
        come = peer(step)
        return pltpu.make_async_remote_copy(
            src_ref=held.at[j, come],
            dst_ref=out_ref.at[:, columns(come * heads + j)],
            send_sem=o_send.at[j, step - 1],
            recv_sem=o_recv.at[j, come],
            device_id=(c, g * group + come),
            device_id_type=MESH,
        )

    def mask_copy(step):
        return pltpu.make_async_remote_copy(
            src_ref=mask_ref,
            dst_ref=masks.at[m],
            send_sem=m_send.at[step - 1],
            recv_sem=m_recv.at[m],
            device_id=(c, g * group + peer(step)),
            device_id_type=MESH,
        )

    def mask_got(step):
        come = peer(step)
        return pltpu.make_async_remote_copy(
            src_ref=mask_ref,
            dst_ref=masks.at[come],
            send_sem=m_send.at[step - 1],
            recv_sem=m_recv.at[come],
            device_id=(c, g * group + come),
            device_id_type=MESH,
        )

    def turned(ref, head):
        x = ref[:, 0, :, columns(head)].astype(jnp.float32).reshape(frames * width, dim)
        y = x * cos_ref[...] + pltpu.roll(x, dim // 2, 1) * sin_ref[...]
        return y.astype(jnp.bfloat16).reshape(frames, width, dim)

    def make_rows(j):
        for step in range(1, group):
            head = peer(step) * heads + j
            rot[head, 0] = turned(k_ref, head)
            rot[head, 1] = v_ref[:, 0, :, columns(head)]
        head = m * heads + j
        ext[j, 0, pl.ds(1, frames), m + 1] = turned(k_ref, head)
        ext[j, 1, pl.ds(1, frames), m + 1] = v_ref[:, 0, :, columns(head)]

    def send_rows(j):
        for step in range(1, group):
            row_copy(j, step, False).start()

    def make_queries(j):
        for step in range(1, group):
            head = peer(step) * heads + j
            q_rot[head] = turned(q_ref, head)
        q_all[j, :, m] = turned(q_ref, m * heads + j)

    def send_queries(j):
        for step in range(1, group):
            query_copy(j, step, False).start()

    def clear(part):
        part[...] = jnp.zeros(part.shape, part.dtype)

    barrier = pltpu.get_barrier_semaphore()
    for step in range(1, group):
        pl.semaphore_signal(barrier, inc=1, device_id=(c, g * group + peer(step)), device_id_type=MESH)
    for dt in range(parts):
        for dg in range(groups):
            if (dt, dg) != (0, 0):
                to = ((c + dt) % parts, (g + dg) % groups * group + m)
                pl.semaphore_signal(barrier, inc=1, device_id=to, device_id_type=MESH)

    loads = [
        pltpu.make_async_copy(src, dst, load.at[n])
        for n, (src, dst) in enumerate(
            [
                (const_hbm, const_ref), (pos_t_hbm, pos_t_ref), (pos_w_hbm, pos_w_ref),
                (mask_hbm, mask_in), (q_hbm, q_ref), (pick_hbm, pick_ref),
            ]
        )
    ]
    def row_load(part, kind, p):
        cols = pl.ds(p * heads * dim, dim) if part == 0 else pl.ds((p * heads + 1) * dim, (heads - 1) * dim)
        src, dst = ((k_hbm, k_ref), (v_hbm, v_ref))[kind]
        return pltpu.make_async_copy(src.at[:, :, :, cols], dst.at[:, :, :, cols], kv_load.at[part, kind, p])

    row_loads = [
        [row_load(part, kind, p) for kind in range(2) for p in range(group)] for part in range(2 if heads > 1 else 1)
    ]
    for copy in loads[:4] + row_loads[0] + sum(row_loads[1:], []) + loads[4:]:
        copy.start()

    pl.when(c == 0)(lambda: clear(ext.at[:, :, 0]))
    pl.when(c == parts - 1)(lambda: clear(ext.at[:, :, frames + 1]))
    pl.when(g == 0)(lambda: clear(ext.at[:, :, :, 0]))
    pl.when(g == groups - 1)(lambda: clear(ext.at[:, :, :, group + 1]))
    clear(mask_pad)

    for copy in loads[:4]:
        copy.wait()

    def column(ref, rows):
        row = ref[...].astype(jnp.float32)
        spread = jnp.broadcast_to(row, (rows, row.shape[1]))
        here = lax.broadcasted_iota(jnp.int32, spread.shape, 0) == lax.broadcasted_iota(jnp.int32, spread.shape, 1)
        return jnp.sum(jnp.where(here, spread, 0.0), axis=1, keepdims=True)

    freq_t = const_ref[width : width + 1, :]
    freq_h = const_ref[width + 1 : width + 2, :]
    freq_w = const_ref[width + 2 : width + 3, :]
    sign = const_ref[width + 3 : width + 4, :]
    pos_h = pos_h_ref[0].astype(jnp.float32)
    angle_hw = pos_h * freq_h + column(pos_w_ref, width) * freq_w
    angle_t = column(pos_t_ref, mask_ref.shape[0]) * freq_t
    for table, of, factor in ((cos_ref, jnp.cos, None), (sin_ref, jnp.sin, sign)):
        of_hw, of_t = of(angle_hw), of(angle_t)
        for f in range(frames):
            part = jnp.where(freq_t > 0, of_t[f : f + 1, :], of_hw)
            table[pl.ds(f * width, width), :] = part if factor is None else part * factor
    slot = mask_ref.shape[1] // mask_in.shape[2]
    for f in range(frames):
        mask_pad[f, pl.ds(0, mask_in.shape[2]), pl.ds(0, mask_in.shape[3])] = (mask_in[f, 0] > 0).astype(jnp.float32)
    clear(mask_ref)
    for f in range(frames):
        tile_rows = mask_pad[f]
        line = tile_rows[0:1, :]
        for b in range(1, mask_in.shape[2]):
            line = line + pltpu.roll(tile_rows, b * slot, 1)[b : b + 1, :]
        mask_ref[f : f + 1, :] = line
    masks[m] = mask_ref[...]

    for copy in row_loads[0]:
        copy.wait()
    make_rows(0)
    pl.semaphore_wait(barrier, group - 1 + parts * groups - 1)
    send_rows(0)
    if heads > 1:
        for copy in row_loads[1]:
            copy.wait()
        make_rows(1)
        send_rows(1)
    if heads > 2:
        make_rows(2)
        send_rows(2)
    for step in range(1, group):
        mask_copy(step).start()

    def spread_on(s):
        for step in range(1, group):
            row_copy(s, step, True).wait_recv()

        @pl.when(c == 0)
        def _():
            for n, to in enumerate(first_targets()):
                first_copy(s, to, g, n).start()

        for n in range(len(NEAR)):
            if n not in CORNERS:
                pl.when(near_here(n, 1))(lambda n=n: near_copy(s, n).start())

        def more_rows():
            make_rows(s + 3)
            send_rows(s + 3)

        def more_queries():
            make_queries(s)
            send_queries(s)

        pl.when(s == 0)(loads[4].wait)
        more_queries()
        pl.when(s + 3 < heads)(more_rows)

        @pl.when(c == 0)
        def _():
            first[s, :, pl.ds(g * group, group)] = ext[s, :, 1, pl.ds(1, group)]

    def make_bias():
        for step in range(1, group):
            mask_got(step).wait_recv()
        loads[5].wait()
        for row in range(group):
            spread = jnp.concatenate(
                [jnp.broadcast_to(masks[row, f : f + 1, :], (width, masks.shape[2])) * const_ref[0:width, :] for f in range(frames)],
                axis=0,
            ).astype(jnp.bfloat16)
            allowed = jnp.dot(spread, pick_ref[row], preferred_element_type=jnp.float32)
            allowed = (allowed - 1.0) * 1e30
            bias[:, pl.ds(row * width, width)] = allowed.reshape(frames, width, allowed.shape[1])

    factor = math.log2(math.e) / math.sqrt(dim)

    def pass_on(j):
        for step in range(1, half):
            first_copy(j, beside(step), beside(step), 0).wait_recv()
        if half < groups:
            pl.when(jnp.logical_not(gate))(lambda: hand_copy(j, 1).wait_recv())
        for to in range(1, parts):
            first_on(j, to).start()

    def send_corners(j):
        for n in ROWS:
            pl.when(near_here(n, -1))(lambda n=n: near_copy(j, n).wait_recv())
        for n in CORNERS:
            pl.when(near_here(n, 1))(lambda n=n: near_copy(j, n).start())

    def attend(j):
        pl.when(c > 0)(lambda: first_on(j, 1).wait_recv())
        for n in range(len(NEAR)):
            if n not in ROWS:
                pl.when(near_here(n, -1))(lambda n=n: near_copy(j, n).wait_recv())

        for step in range(1, group):
            query_copy(j, step, True).wait_recv()
        far_k = first[j, 0].reshape(-1, dim)
        far_v = first[j, 1].reshape(-1, dim)
        far_v = jnp.concatenate([far_v, jnp.ones_like(far_v)], axis=1)
        last = (((1,), (1,)), ((), ()))
        s_all = lax.dot_general(
            q_all[j].reshape(frames * tokens, dim), far_k, last, preferred_element_type=jnp.float32
        )
        near, p_all = [], []
        for f in range(frames):
            q = q_all[j, f].reshape(tokens, dim)
            near_k = ext[j, 0, pl.ds(f, 3)].reshape(-1, dim)
            near_v = ext[j, 1, pl.ds(f, 3)].reshape(-1, dim)
            near_v = jnp.concatenate([near_v, jnp.ones_like(near_v)], axis=1)
            s_near = lax.dot_general(q, near_k, last, preferred_element_type=jnp.float32) + bias[f]
            s_far = s_all[f * tokens : (f + 1) * tokens]
            top = jnp.maximum(
                jnp.max(s_near, axis=1, keepdims=True), jnp.max(s_far, axis=1, keepdims=True)
            )
            p_near = jnp.exp2((s_near - top) * factor).astype(jnp.bfloat16)
            p_all.append(jnp.exp2((s_far - top) * factor).astype(jnp.bfloat16))
            near.append(jnp.dot(p_near, near_v, preferred_element_type=jnp.float32))
        far = jnp.dot(jnp.concatenate(p_all, axis=0), far_v, preferred_element_type=jnp.float32)
        for f in range(frames):
            both = near[f] + far[f * tokens : (f + 1) * tokens]
            result = (both[:, :dim] / both[:, dim:]).astype(jnp.bfloat16)
            held[j, :, pl.ds(f * width, width)] = result.reshape(group, width, dim)
        for step in range(1, group):
            out_copy(j, step).start()
        out_ref[:, columns(m * heads + j)] = held[j, m]

    def turn(s, carry):
        pl.when(s < heads)(lambda: spread_on(s))
        pl.when(s == 0)(make_bias)
        if half < groups:
            pl.when((c == 0) & gate & (s > 0) & (s <= heads))(lambda: hand_on(s - 1))
        pl.when(s > 1)(lambda: attend(s - 2))
        pl.when((s > 0) & (s <= heads))(lambda: send_corners(s - 1))
        pl.when((c == 0) & (s > 0) & (s <= heads))(lambda: pass_on(s - 1))
        return carry

    lax.fori_loop(0, heads + 2, turn, 0)

    def finish(j, carry):
        for step in range(1, group):
            row_copy(j, step, False).wait_send()
            query_copy(j, step, False).wait_send()
            out_copy(j, step).wait_send()
            out_got(j, step).wait_recv()
        for n in range(len(NEAR)):
            pl.when(near_here(n, 1))(lambda n=n: near_copy(j, n).wait_send())

        @pl.when(c == 0)
        def _():
            for n, to in enumerate(first_targets()):
                first_copy(j, to, g, n).wait_send()
            for to in range(1, parts):
                first_on(j, to).wait_send()

        if half < groups:

            @pl.when((c == 0) & gate)
            def _():
                for step in range(1, half):
                    hand_copy(j, step).wait_send()

        return carry

    lax.fori_loop(0, heads, finish, 0)
    for step in range(1, group):
        mask_copy(step).wait_send()


def per_device(parts, high, queries, keys, values, window_mask, pos_t, pos_h, pos_w):
    frames, row_count, width, channels = queries.shape
    assert row_count == 1
    dim = HEAD_DIM
    group = next(n for n in (4, 2, 1) if HEADS % n == 0 and high % n == 0)
    groups, heads = high // group, HEADS // group
    blocks = width // TILE_W
    lanes = 128
    tokens = frames * width
    mask_rows = -(-frames // 8) * 8
    own, pick = mask_selectors(group, width, lanes)
    const = np.concatenate([own, frequencies(dim // 2)], axis=0)
    const = np.pad(const, ((0, -len(const) % 8), (0, 0)))
    keys_near = pick.shape[2]
    sem = pltpu.SemaphoreType.DMA
    in_hbm = functools.partial(pltpu.with_memory_space_constraint, memory_space=pltpu.HBM)
    out = pl.pallas_call(
        functools.partial(kernel, (group, groups, parts, frames, width, heads)),
        out_shape=jax.ShapeDtypeStruct((tokens, channels), jnp.bfloat16),
        in_specs=[pl.BlockSpec(memory_space=pltpu.SMEM if n == 5 else pltpu.HBM) for n in range(9)],
        out_specs=pl.BlockSpec(memory_space=pltpu.VMEM),
        scratch_shapes=[
            pltpu.VMEM(queries.shape, jnp.bfloat16),
            pltpu.VMEM(queries.shape, jnp.bfloat16),
            pltpu.VMEM(queries.shape, jnp.bfloat16),
            pltpu.VMEM(window_mask.shape, jnp.int32),
            pltpu.VMEM((1, frames), jnp.int32),
            pltpu.VMEM((1, width), jnp.int32),
            pltpu.VMEM(const.shape, jnp.float32),
            pltpu.VMEM(pick.shape, jnp.bfloat16),
            pltpu.VMEM((tokens, dim), jnp.float32),
            pltpu.VMEM((tokens, dim), jnp.float32),
            pltpu.VMEM((frames, -(-blocks // 8) * 8, lanes), jnp.float32),
            pltpu.VMEM((mask_rows, lanes), jnp.float32),
            pltpu.VMEM((HEADS, frames, width, dim), jnp.bfloat16),
            pltpu.VMEM((HEADS, 2, frames, width, dim), jnp.bfloat16),
            pltpu.VMEM((heads, frames, group, width, dim), jnp.bfloat16),
            pltpu.VMEM((heads, 2, frames + 2, group + 2, width, dim), jnp.bfloat16),
            pltpu.VMEM((heads, 2, high, width, dim), jnp.bfloat16),
            pltpu.VMEM((heads, group, tokens, dim), jnp.bfloat16),
            pltpu.VMEM((group, mask_rows, lanes), jnp.float32),
            pltpu.VMEM((frames, group * width, keys_near), jnp.float32),
            sem((6,)),
            sem((2, 2, group)),
            sem((heads, max(1, group - 1))),
            sem((heads, group)),
            sem((heads, max(1, group - 1))),
            sem((heads, group)),
            sem((heads, len(NEAR))),
            sem((heads, len(NEAR))),
            sem((heads, max(1, groups - 1))),
            sem((heads, groups)),
            sem((heads, max(1, groups - 1))),
            sem((heads,)),
            sem((heads, max(1, parts - 1))),
            sem((heads,)),
            sem((heads, max(1, group - 1))),
            sem((heads, group)),
            sem((max(1, group - 1),)),
            sem((group,)),
        ],
        compiler_params=pltpu.CompilerParams(
            collective_id=0, has_side_effects=True, vmem_limit_bytes=48 * 1024 * 1024
        ),
    )(
        *(in_hbm(x) for x in (queries, keys, values, window_mask)),
        in_hbm(pos_t.reshape(1, -1)),
        pos_h,
        in_hbm(pos_w.reshape(1, -1)),
        in_hbm(jnp.asarray(const)),
        in_hbm(jnp.asarray(pick, jnp.bfloat16)),
    )
    return out.reshape(queries.shape)


def solution(mesh):
    return jax.shard_map(
        functools.partial(per_device, mesh.shape["tm"], mesh.shape["height"]),
        mesh=mesh,
        in_specs=(
            P("tm", "height", None, None),
            P("tm", "height", None, None),
            P("tm", "height", None, None),
            P("tm", "height", None, None),
            P("tm"),
            P("height"),
            P(),
        ),
        out_specs=P("tm", "height", None, None),
        check_vma=False,
    )
```

```python
import functools
import math

import jax
import jax.numpy as jnp
import numpy as np
from jax import lax
from jax.experimental import pallas as pl
from jax.experimental.pallas import tpu as pltpu
from jax.sharding import PartitionSpec as P

HEADS = 20
HEAD_DIM = 128
TILE_W = 8
MESH = pl.DeviceIdType.MESH
NEAR = [(dc, dg) for dc in (-1, 0, 1) for dg in (-1, 0, 1) if (dc, dg) != (0, 0)]


def frequencies(half_dim):
    pairs_hw = 2 * half_dim // 6
    pairs_time = half_dim - 2 * pairs_hw
    pair = np.arange(2 * half_dim) % half_dim
    count = np.where(pair < pairs_time, pairs_time, pairs_hw)
    first = np.where(pair < pairs_time, 0, np.where(pair < pairs_time + pairs_hw, pairs_time, pairs_time + pairs_hw))
    freq = 10000.0 ** (-(pair - first) / count)
    sign = np.where(np.arange(2 * half_dim) < half_dim, -1.0, 1.0)
    rows = [np.where(first == start, freq, 0.0) for start in (0, pairs_time, pairs_time + pairs_hw)]
    return np.stack(rows + [sign]).astype(np.float32)


def mask_selectors(group, width, lanes):
    blocks = width // TILE_W
    slot = lanes // blocks
    keys = 3 * (group + 2) * width
    own = (np.arange(width)[:, None] // TILE_W == np.arange(lanes)[None, :] // slot)
    key = np.arange(keys)
    step_t = key // ((group + 2) * width)
    key_row = key // width % (group + 2)
    key_block = key % width // TILE_W
    pick = np.zeros((group, lanes, keys), np.float32)
    for row in range(group):
        for block in range(blocks):
            step_h = key_row - row
            step_w = key_block - block + 1
            inside = (step_h >= 0) & (step_h < 3) & (step_w >= 0) & (step_w < 3)
            offset = step_t * 9 + step_h * 3 + step_w
            pick[row, (block * slot + offset)[inside], key[inside]] = 1.0
    return own.astype(np.float32), pick


def kernel(
    sizes, q_hbm, k_hbm, v_hbm, mask_hbm, pos_t_hbm, pos_h_ref, pos_w_hbm, const_hbm, pick_hbm, out_ref,
    q_ref, k_ref, v_ref, mask_in, pos_t_ref, pos_w_ref, const_ref, pick_ref,
    cos_ref, sin_ref, mask_pad, mask_ref, q_rot, rot, q_all, ext, first, held, masks, bias,
    load, kv_load, q_send, q_recv, a_send, a_recv, n_send, n_recv, f_send, f_recv, t_send, t_recv, o_send, o_recv, m_send, m_recv,
):
    group, groups, parts, frames, width, heads = sizes
    dim = HEAD_DIM
    tokens = group * width
    c = lax.axis_index("tm")
    at = lax.axis_index("height")
    g = at // group
    m = at % group

    def peer(step):
        return (m + step) % group

    def row_copy(j, step, landing):
        other = peer(step)
        row = other if landing else m
        return pltpu.make_async_remote_copy(
            src_ref=rot.at[other * heads + j],
            dst_ref=ext.at[j, :, pl.ds(1, frames), row + 1],
            send_sem=a_send.at[j, step - 1],
            recv_sem=a_recv.at[j, row],
            device_id=(c, g * group + other),
            device_id_type=MESH,
        )

    def query_copy(j, step, landing):
        other = peer(step)
        row = other if landing else m
        return pltpu.make_async_remote_copy(
            src_ref=q_rot.at[other * heads + j],
            dst_ref=q_all.at[j, :, row],
            send_sem=q_send.at[j, step - 1],
            recv_sem=q_recv.at[j, row],
            device_id=(c, g * group + other),
            device_id_type=MESH,
        )

    def near_copy(j, n):
        dc, dg = NEAR[n]
        src_t = {-1: pl.ds(1, 1), 0: pl.ds(1, frames), 1: pl.ds(frames, 1)}[dc]
        dst_t = {-1: pl.ds(frames + 1, 1), 0: pl.ds(1, frames), 1: pl.ds(0, 1)}[dc]
        src_h = {-1: pl.ds(1, 1), 0: pl.ds(1, group), 1: pl.ds(group, 1)}[dg]
        dst_h = {-1: pl.ds(group + 1, 1), 0: pl.ds(1, group), 1: pl.ds(0, 1)}[dg]
        return pltpu.make_async_remote_copy(
            src_ref=ext.at[j, :, src_t, src_h],
            dst_ref=ext.at[j, :, dst_t, dst_h],
            send_sem=n_send.at[j, n],
            recv_sem=n_recv.at[j, n],
            device_id=(c + dc, at + dg * group),
            device_id_type=MESH,
        )

    def near_here(n, sign):
        dc, dg = sign * NEAR[n][0], sign * NEAR[n][1]
        ok = (c + dc >= 0) & (c + dc < parts)
        return ok & (g + dg >= 0) & (g + dg < groups)

    def first_copy(j, step):
        to = (g + step) % groups
        return pltpu.make_async_remote_copy(
            src_ref=ext.at[j, :, 1, pl.ds(1, group)],
            dst_ref=first.at[j, :, pl.ds(g * group, group)],
            send_sem=f_send.at[j, step - 1],
            recv_sem=f_recv.at[j, g],
            device_id=(c, to * group + m),
            device_id_type=MESH,
        )

    def first_got(j, step):
        come = (g + step) % groups
        return pltpu.make_async_remote_copy(
            src_ref=ext.at[j, :, 1, pl.ds(1, group)],
            dst_ref=first.at[j, :, pl.ds(come * group, group)],
            send_sem=f_send.at[j, step - 1],
            recv_sem=f_recv.at[j, come],
            device_id=(c, come * group + m),
            device_id_type=MESH,
        )

    def first_on(j, to):
        return pltpu.make_async_remote_copy(
            src_ref=first.at[j],
            dst_ref=first.at[j],
            send_sem=t_send.at[j, to - 1],
            recv_sem=t_recv.at[j],
            device_id=(to, at),
            device_id_type=MESH,
        )

    def columns(head):
        return pl.ds(pl.multiple_of(head * dim, dim), dim)

    def out_copy(j, step):
        to = peer(step)
        return pltpu.make_async_remote_copy(
            src_ref=held.at[j, to],
            dst_ref=out_ref.at[:, columns(m * heads + j)],
            send_sem=o_send.at[j, step - 1],
            recv_sem=o_recv.at[j, m],
            device_id=(c, g * group + to),
            device_id_type=MESH,
        )

    def out_got(j, step):
        come = peer(step)
        return pltpu.make_async_remote_copy(
            src_ref=held.at[j, come],
            dst_ref=out_ref.at[:, columns(come * heads + j)],
            send_sem=o_send.at[j, step - 1],
            recv_sem=o_recv.at[j, come],
            device_id=(c, g * group + come),
            device_id_type=MESH,
        )

    def mask_copy(step):
        return pltpu.make_async_remote_copy(
            src_ref=mask_ref,
            dst_ref=masks.at[m],
            send_sem=m_send.at[step - 1],
            recv_sem=m_recv.at[m],
            device_id=(c, g * group + peer(step)),
            device_id_type=MESH,
        )

    def mask_got(step):
        come = peer(step)
        return pltpu.make_async_remote_copy(
            src_ref=mask_ref,
            dst_ref=masks.at[come],
            send_sem=m_send.at[step - 1],
            recv_sem=m_recv.at[come],
            device_id=(c, g * group + come),
            device_id_type=MESH,
        )

    def turned(ref, head):
        x = ref[:, 0, :, columns(head)].astype(jnp.float32).reshape(frames * width, dim)
        y = x * cos_ref[...] + pltpu.roll(x, dim // 2, 1) * sin_ref[...]
        return y.astype(jnp.bfloat16).reshape(frames, width, dim)

    def make_rows(j):
        for step in range(1, group):
            head = peer(step) * heads + j
            rot[head, 0] = turned(k_ref, head)
            rot[head, 1] = v_ref[:, 0, :, columns(head)]
        head = m * heads + j
        ext[j, 0, pl.ds(1, frames), m + 1] = turned(k_ref, head)
        ext[j, 1, pl.ds(1, frames), m + 1] = v_ref[:, 0, :, columns(head)]

    def send_rows(j):
        for step in range(1, group):
            row_copy(j, step, False).start()

    def rows_left(j):
        for step in range(1, group):
            row_copy(j, step, False).wait_send()

    def make_queries(j):
        for step in range(1, group):
            head = peer(step) * heads + j
            q_rot[head] = turned(q_ref, head)
        q_all[j, :, m] = turned(q_ref, m * heads + j)

    def send_queries(j):
        for step in range(1, group):
            query_copy(j, step, False).start()

    def clear(part):
        part[...] = jnp.zeros(part.shape, part.dtype)

    barrier = pltpu.get_barrier_semaphore()
    for step in range(1, group):
        pl.semaphore_signal(barrier, inc=1, device_id=(c, g * group + peer(step)), device_id_type=MESH)
    for dt in range(parts):
        for dg in range(groups):
            if (dt, dg) != (0, 0):
                to = ((c + dt) % parts, (g + dg) % groups * group + m)
                pl.semaphore_signal(barrier, inc=1, device_id=to, device_id_type=MESH)

    loads = [
        pltpu.make_async_copy(src, dst, load.at[n])
        for n, (src, dst) in enumerate(
            [
                (const_hbm, const_ref), (pos_t_hbm, pos_t_ref), (pos_w_hbm, pos_w_ref),
                (mask_hbm, mask_in), (q_hbm, q_ref), (pick_hbm, pick_ref),
            ]
        )
    ]
    def row_load(part, kind, p):
        cols = pl.ds(p * heads * dim, dim) if part == 0 else pl.ds((p * heads + 1) * dim, (heads - 1) * dim)
        src, dst = ((k_hbm, k_ref), (v_hbm, v_ref))[kind]
        return pltpu.make_async_copy(src.at[:, :, :, cols], dst.at[:, :, :, cols], kv_load.at[part, kind, p])

    row_loads = [
        [row_load(part, kind, p) for kind in range(2) for p in range(group)] for part in range(2 if heads > 1 else 1)
    ]
    for copy in loads[:4] + row_loads[0] + sum(row_loads[1:], []) + loads[4:]:
        copy.start()

    pl.when(c == 0)(lambda: clear(ext.at[:, :, 0]))
    pl.when(c == parts - 1)(lambda: clear(ext.at[:, :, frames + 1]))
    pl.when(g == 0)(lambda: clear(ext.at[:, :, :, 0]))
    pl.when(g == groups - 1)(lambda: clear(ext.at[:, :, :, group + 1]))
    clear(mask_pad)

    for copy in loads[:4]:
        copy.wait()

    def column(ref, rows):
        row = ref[...].astype(jnp.float32)
        spread = jnp.broadcast_to(row, (rows, row.shape[1]))
        here = lax.broadcasted_iota(jnp.int32, spread.shape, 0) == lax.broadcasted_iota(jnp.int32, spread.shape, 1)
        return jnp.sum(jnp.where(here, spread, 0.0), axis=1, keepdims=True)

    freq_t = const_ref[width : width + 1, :]
    freq_h = const_ref[width + 1 : width + 2, :]
    freq_w = const_ref[width + 2 : width + 3, :]
    sign = const_ref[width + 3 : width + 4, :]
    pos_h = pos_h_ref[0].astype(jnp.float32)
    angle_hw = pos_h * freq_h + column(pos_w_ref, width) * freq_w
    angle_t = column(pos_t_ref, mask_ref.shape[0]) * freq_t
    for table, of, factor in ((cos_ref, jnp.cos, None), (sin_ref, jnp.sin, sign)):
        of_hw, of_t = of(angle_hw), of(angle_t)
        for f in range(frames):
            part = jnp.where(freq_t > 0, of_t[f : f + 1, :], of_hw)
            table[pl.ds(f * width, width), :] = part if factor is None else part * factor
    slot = mask_ref.shape[1] // mask_in.shape[2]
    for f in range(frames):
        mask_pad[f, pl.ds(0, mask_in.shape[2]), pl.ds(0, mask_in.shape[3])] = (mask_in[f, 0] > 0).astype(jnp.float32)
    clear(mask_ref)
    for f in range(frames):
        tile_rows = mask_pad[f]
        line = tile_rows[0:1, :]
        for b in range(1, mask_in.shape[2]):
            line = line + pltpu.roll(tile_rows, b * slot, 1)[b : b + 1, :]
        mask_ref[f : f + 1, :] = line
    masks[m] = mask_ref[...]

    for copy in row_loads[0]:
        copy.wait()
    make_rows(0)
    pl.semaphore_wait(barrier, group - 1 + parts * groups - 1)
    send_rows(0)
    if heads > 1:
        for copy in row_loads[1]:
            copy.wait()
        make_rows(1)
        rows_left(0)
        send_rows(1)
    for step in range(1, group):
        mask_copy(step).start()

    def spread_on(s):
        for step in range(1, group):
            row_copy(s, step, True).wait_recv()

        @pl.when(c == 0)
        def _():
            for step in range(1, groups):
                first_copy(s, step).start()

        for n in range(len(NEAR)):
            pl.when(near_here(n, 1))(lambda n=n: near_copy(s, n).start())

        def more_rows():
            make_rows(s + 2)
            rows_left(s + 1)
            send_rows(s + 2)

        def more_queries():
            make_queries(s)
            send_queries(s)

        pl.when(s == 0)(loads[4].wait)
        pl.when(s + 2 < heads)(more_rows)
        more_queries()

        @pl.when(c == 0)
        def _():
            first[s, :, pl.ds(g * group, group)] = ext[s, :, 1, pl.ds(1, group)]

    def make_bias():
        for step in range(1, group):
            mask_got(step).wait_recv()
        loads[5].wait()
        for row in range(group):
            spread = jnp.concatenate(
                [jnp.broadcast_to(masks[row, f : f + 1, :], (width, masks.shape[2])) * const_ref[0:width, :] for f in range(frames)],
                axis=0,
            ).astype(jnp.bfloat16)
            allowed = jnp.dot(spread, pick_ref[row], preferred_element_type=jnp.float32)
            allowed = (allowed - 1.0) * 1e30
            bias[:, pl.ds(row * width, width)] = allowed.reshape(frames, width, allowed.shape[1])

    factor = math.log2(math.e) / math.sqrt(dim)

    def pass_on(j):
        for step in range(1, groups):
            first_got(j, step).wait_recv()
        for to in range(1, parts):
            first_on(j, to).start()

    def attend(j):
        pl.when(c > 0)(lambda: first_on(j, 1).wait_recv())
        for n in range(len(NEAR)):
            pl.when(near_here(n, -1))(lambda n=n: near_copy(j, n).wait_recv())

        for step in range(1, group):
            query_copy(j, step, True).wait_recv()
        far_k = first[j, 0].reshape(-1, dim)
        far_v = first[j, 1].reshape(-1, dim)
        far_v = jnp.concatenate([far_v, jnp.ones_like(far_v)], axis=1)
        last = (((1,), (1,)), ((), ()))
        s_all = lax.dot_general(
            q_all[j].reshape(frames * tokens, dim), far_k, last, preferred_element_type=jnp.float32
        )
        near, p_all = [], []
        for f in range(frames):
            q = q_all[j, f].reshape(tokens, dim)
            near_k = ext[j, 0, pl.ds(f, 3)].reshape(-1, dim)
            near_v = ext[j, 1, pl.ds(f, 3)].reshape(-1, dim)
            near_v = jnp.concatenate([near_v, jnp.ones_like(near_v)], axis=1)
            s_near = lax.dot_general(q, near_k, last, preferred_element_type=jnp.float32) + bias[f]
            s_far = s_all[f * tokens : (f + 1) * tokens]
            top = jnp.maximum(
                jnp.max(s_near, axis=1, keepdims=True), jnp.max(s_far, axis=1, keepdims=True)
            )
            p_near = jnp.exp2((s_near - top) * factor).astype(jnp.bfloat16)
            p_all.append(jnp.exp2((s_far - top) * factor).astype(jnp.bfloat16))
            near.append(jnp.dot(p_near, near_v, preferred_element_type=jnp.float32))
        far = jnp.dot(jnp.concatenate(p_all, axis=0), far_v, preferred_element_type=jnp.float32)
        for f in range(frames):
            both = near[f] + far[f * tokens : (f + 1) * tokens]
            result = (both[:, :dim] / both[:, dim:]).astype(jnp.bfloat16)
            held[j, :, pl.ds(f * width, width)] = result.reshape(group, width, dim)
        for step in range(1, group):
            out_copy(j, step).start()
        out_ref[:, columns(m * heads + j)] = held[j, m]

    def turn(s, carry):
        pl.when(s < heads)(lambda: spread_on(s))
        pl.when(s == 0)(make_bias)
        pl.when(s > 1)(lambda: attend(s - 2))
        pl.when((c == 0) & (s > 0) & (s <= heads))(lambda: pass_on(s - 1))
        return carry

    lax.fori_loop(0, heads + 2, turn, 0)

    rows_left(heads - 1)

    def finish(j, carry):
        for step in range(1, group):
            query_copy(j, step, False).wait_send()
            out_copy(j, step).wait_send()
            out_got(j, step).wait_recv()
        for n in range(len(NEAR)):
            pl.when(near_here(n, 1))(lambda n=n: near_copy(j, n).wait_send())

        @pl.when(c == 0)
        def _():
            for step in range(1, groups):
                first_copy(j, step).wait_send()
            for to in range(1, parts):
                first_on(j, to).wait_send()

        return carry

    lax.fori_loop(0, heads, finish, 0)
    for step in range(1, group):
        mask_copy(step).wait_send()


def per_device(parts, high, queries, keys, values, window_mask, pos_t, pos_h, pos_w):
    frames, row_count, width, channels = queries.shape
    assert row_count == 1
    dim = HEAD_DIM
    group = next(n for n in (4, 2, 1) if HEADS % n == 0 and high % n == 0)
    groups, heads = high // group, HEADS // group
    blocks = width // TILE_W
    lanes = 128
    tokens = frames * width
    mask_rows = -(-frames // 8) * 8
    own, pick = mask_selectors(group, width, lanes)
    const = np.concatenate([own, frequencies(dim // 2)], axis=0)
    const = np.pad(const, ((0, -len(const) % 8), (0, 0)))
    keys_near = pick.shape[2]
    sem = pltpu.SemaphoreType.DMA
    in_hbm = functools.partial(pltpu.with_memory_space_constraint, memory_space=pltpu.HBM)
    out = pl.pallas_call(
        functools.partial(kernel, (group, groups, parts, frames, width, heads)),
        out_shape=jax.ShapeDtypeStruct((tokens, channels), jnp.bfloat16),
        in_specs=[pl.BlockSpec(memory_space=pltpu.SMEM if n == 5 else pltpu.HBM) for n in range(9)],
        out_specs=pl.BlockSpec(memory_space=pltpu.VMEM),
        scratch_shapes=[
            pltpu.VMEM(queries.shape, jnp.bfloat16),
            pltpu.VMEM(queries.shape, jnp.bfloat16),
            pltpu.VMEM(queries.shape, jnp.bfloat16),
            pltpu.VMEM(window_mask.shape, jnp.int32),
            pltpu.VMEM((1, frames), jnp.int32),
            pltpu.VMEM((1, width), jnp.int32),
            pltpu.VMEM(const.shape, jnp.float32),
            pltpu.VMEM(pick.shape, jnp.bfloat16),
            pltpu.VMEM((tokens, dim), jnp.float32),
            pltpu.VMEM((tokens, dim), jnp.float32),
            pltpu.VMEM((frames, -(-blocks // 8) * 8, lanes), jnp.float32),
            pltpu.VMEM((mask_rows, lanes), jnp.float32),
            pltpu.VMEM((HEADS, frames, width, dim), jnp.bfloat16),
            pltpu.VMEM((HEADS, 2, frames, width, dim), jnp.bfloat16),
            pltpu.VMEM((heads, frames, group, width, dim), jnp.bfloat16),
            pltpu.VMEM((heads, 2, frames + 2, group + 2, width, dim), jnp.bfloat16),
            pltpu.VMEM((heads, 2, high, width, dim), jnp.bfloat16),
            pltpu.VMEM((heads, group, tokens, dim), jnp.bfloat16),
            pltpu.VMEM((group, mask_rows, lanes), jnp.float32),
            pltpu.VMEM((frames, group * width, keys_near), jnp.float32),
            sem((6,)),
            sem((2, 2, group)),
            sem((heads, max(1, group - 1))),
            sem((heads, group)),
            sem((heads, max(1, group - 1))),
            sem((heads, group)),
            sem((heads, len(NEAR))),
            sem((heads, len(NEAR))),
            sem((heads, max(1, groups - 1))),
            sem((heads, groups)),
            sem((heads, max(1, parts - 1))),
            sem((heads,)),
            sem((heads, max(1, group - 1))),
            sem((heads, group)),
            sem((max(1, group - 1),)),
            sem((group,)),
        ],
        compiler_params=pltpu.CompilerParams(
            collective_id=0, has_side_effects=True, vmem_limit_bytes=48 * 1024 * 1024
        ),
    )(
        *(in_hbm(x) for x in (queries, keys, values, window_mask)),
        in_hbm(pos_t.reshape(1, -1)),
        pos_h,
        in_hbm(pos_w.reshape(1, -1)),
        in_hbm(jnp.asarray(const)),
        in_hbm(jnp.asarray(pick, jnp.bfloat16)),
    )
    return out.reshape(queries.shape)


def solution(mesh):
    return jax.shard_map(
        functools.partial(per_device, mesh.shape["tm"], mesh.shape["height"]),
        mesh=mesh,
        in_specs=(
            P("tm", "height", None, None),
            P("tm", "height", None, None),
            P("tm", "height", None, None),
            P("tm", "height", None, None),
            P("tm"),
            P("height"),
            P(),
        ),
        out_specs=P("tm", "height", None, None),
        check_vma=False,
    )
```

```python
import functools
import math

import jax
import jax.numpy as jnp
import numpy as np
from jax import lax
from jax.experimental import pallas as pl
from jax.experimental.pallas import tpu as pltpu
from jax.sharding import PartitionSpec as P

HEADS = 20
HEAD_DIM = 128
TILE_W = 8
MESH = pl.DeviceIdType.MESH
NEAR = [(dc, dg) for dc in (-1, 0, 1) for dg in (-1, 0, 1) if (dc, dg) != (0, 0)]


def frequencies(half_dim):
    pairs_hw = 2 * half_dim // 6
    pairs_time = half_dim - 2 * pairs_hw
    pair = np.arange(2 * half_dim) % half_dim
    count = np.where(pair < pairs_time, pairs_time, pairs_hw)
    first = np.where(pair < pairs_time, 0, np.where(pair < pairs_time + pairs_hw, pairs_time, pairs_time + pairs_hw))
    freq = 10000.0 ** (-(pair - first) / count)
    sign = np.where(np.arange(2 * half_dim) < half_dim, -1.0, 1.0)
    rows = [np.where(first == start, freq, 0.0) for start in (0, pairs_time, pairs_time + pairs_hw)]
    return np.stack(rows + [sign]).astype(np.float32)


def mask_selectors(group, width, lanes):
    blocks = width // TILE_W
    slot = lanes // blocks
    keys = 3 * (group + 2) * width
    own = (np.arange(width)[:, None] // TILE_W == np.arange(lanes)[None, :] // slot)
    key = np.arange(keys)
    step_t = key // ((group + 2) * width)
    key_row = key // width % (group + 2)
    key_block = key % width // TILE_W
    pick = np.zeros((group, lanes, keys), np.float32)
    for row in range(group):
        for block in range(blocks):
            step_h = key_row - row
            step_w = key_block - block + 1
            inside = (step_h >= 0) & (step_h < 3) & (step_w >= 0) & (step_w < 3)
            offset = step_t * 9 + step_h * 3 + step_w
            pick[row, (block * slot + offset)[inside], key[inside]] = 1.0
    return own.astype(np.float32), pick


def kernel(
    sizes, q_hbm, k_hbm, v_hbm, mask_hbm, pos_t_hbm, pos_h_ref, pos_w_hbm, const_hbm, pick_hbm, out_ref,
    q_ref, k_ref, v_ref, mask_in, pos_t_ref, pos_w_ref, const_ref, pick_ref,
    cos_ref, sin_ref, mask_pad, mask_ref, q_rot, rot, q_all, ext, first, held, masks, bias,
    load, kv_load, q_send, q_recv, a_send, a_recv, n_send, n_recv, f_send, f_recv, t_send, t_recv, o_send, o_recv, m_send, m_recv,
):
    group, groups, parts, frames, width, heads = sizes
    dim = HEAD_DIM
    tokens = group * width
    c = lax.axis_index("tm")
    at = lax.axis_index("height")
    g = at // group
    m = at % group

    def peer(step):
        return (m + step) % group

    def row_copy(j, step, landing):
        other = peer(step)
        row = other if landing else m
        return pltpu.make_async_remote_copy(
            src_ref=rot.at[other * heads + j],
            dst_ref=ext.at[j, :, pl.ds(1, frames), row + 1],
            send_sem=a_send.at[j, step - 1],
            recv_sem=a_recv.at[j, row],
            device_id=(c, g * group + other),
            device_id_type=MESH,
        )

    def query_copy(j, step, landing):
        other = peer(step)
        row = other if landing else m
        return pltpu.make_async_remote_copy(
            src_ref=q_rot.at[other * heads + j],
            dst_ref=q_all.at[j, :, row],
            send_sem=q_send.at[j, step - 1],
            recv_sem=q_recv.at[j, row],
            device_id=(c, g * group + other),
            device_id_type=MESH,
        )

    def near_copy(j, n):
        dc, dg = NEAR[n]
        src_t = {-1: pl.ds(1, 1), 0: pl.ds(1, frames), 1: pl.ds(frames, 1)}[dc]
        dst_t = {-1: pl.ds(frames + 1, 1), 0: pl.ds(1, frames), 1: pl.ds(0, 1)}[dc]
        src_h = {-1: pl.ds(1, 1), 0: pl.ds(1, group), 1: pl.ds(group, 1)}[dg]
        dst_h = {-1: pl.ds(group + 1, 1), 0: pl.ds(1, group), 1: pl.ds(0, 1)}[dg]
        return pltpu.make_async_remote_copy(
            src_ref=ext.at[j, :, src_t, src_h],
            dst_ref=ext.at[j, :, dst_t, dst_h],
            send_sem=n_send.at[j, n],
            recv_sem=n_recv.at[j, n],
            device_id=(c + dc, at + dg * group),
            device_id_type=MESH,
        )

    def near_here(n, sign):
        dc, dg = sign * NEAR[n][0], sign * NEAR[n][1]
        ok = (c + dc >= 0) & (c + dc < parts)
        return ok & (g + dg >= 0) & (g + dg < groups)

    def first_copy(j, step):
        to = (g + step) % groups
        return pltpu.make_async_remote_copy(
            src_ref=ext.at[j, :, 1, pl.ds(1, group)],
            dst_ref=first.at[j, :, pl.ds(g * group, group)],
            send_sem=f_send.at[j, step - 1],
            recv_sem=f_recv.at[j, g],
            device_id=(c, to * group + m),
            device_id_type=MESH,
        )

    def first_got(j, step):
        come = (g + step) % groups
        return pltpu.make_async_remote_copy(
            src_ref=ext.at[j, :, 1, pl.ds(1, group)],
            dst_ref=first.at[j, :, pl.ds(come * group, group)],
            send_sem=f_send.at[j, step - 1],
            recv_sem=f_recv.at[j, come],
            device_id=(c, come * group + m),
            device_id_type=MESH,
        )

    def first_on(j, to):
        return pltpu.make_async_remote_copy(
            src_ref=first.at[j],
            dst_ref=first.at[j],
            send_sem=t_send.at[j, to - 1],
            recv_sem=t_recv.at[j],
            device_id=(to, at),
            device_id_type=MESH,
        )

    def columns(head):
        return pl.ds(pl.multiple_of(head * dim, dim), dim)

    def out_copy(j, step):
        to = peer(step)
        return pltpu.make_async_remote_copy(
            src_ref=held.at[j, to],
            dst_ref=out_ref.at[:, columns(m * heads + j)],
            send_sem=o_send.at[j, step - 1],
            recv_sem=o_recv.at[j, m],
            device_id=(c, g * group + to),
            device_id_type=MESH,
        )

    def out_got(j, step):
        come = peer(step)
        return pltpu.make_async_remote_copy(
            src_ref=held.at[j, come],
            dst_ref=out_ref.at[:, columns(come * heads + j)],
            send_sem=o_send.at[j, step - 1],
            recv_sem=o_recv.at[j, come],
            device_id=(c, g * group + come),
            device_id_type=MESH,
        )

    def mask_copy(step):
        return pltpu.make_async_remote_copy(
            src_ref=mask_ref,
            dst_ref=masks.at[m],
            send_sem=m_send.at[step - 1],
            recv_sem=m_recv.at[m],
            device_id=(c, g * group + peer(step)),
            device_id_type=MESH,
        )

    def mask_got(step):
        come = peer(step)
        return pltpu.make_async_remote_copy(
            src_ref=mask_ref,
            dst_ref=masks.at[come],
            send_sem=m_send.at[step - 1],
            recv_sem=m_recv.at[come],
            device_id=(c, g * group + come),
            device_id_type=MESH,
        )

    def turned(ref, head):
        x = ref[:, 0, :, columns(head)].astype(jnp.float32).reshape(frames * width, dim)
        y = x * cos_ref[...] + pltpu.roll(x, dim // 2, 1) * sin_ref[...]
        return y.astype(jnp.bfloat16).reshape(frames, width, dim)

    def make_rows(j):
        for step in range(1, group):
            head = peer(step) * heads + j
            rot[head, 0] = turned(k_ref, head)
            rot[head, 1] = v_ref[:, 0, :, columns(head)]
        head = m * heads + j
        ext[j, 0, pl.ds(1, frames), m + 1] = turned(k_ref, head)
        ext[j, 1, pl.ds(1, frames), m + 1] = v_ref[:, 0, :, columns(head)]

    def send_rows(j):
        for step in range(1, group):
            row_copy(j, step, False).start()

    def rows_left(j):
        for step in range(1, group):
            row_copy(j, step, False).wait_send()

    def make_queries(j):
        for step in range(1, group):
            head = peer(step) * heads + j
            q_rot[head] = turned(q_ref, head)
        q_all[j, :, m] = turned(q_ref, m * heads + j)

    def send_queries(j):
        for step in range(1, group):
            query_copy(j, step, False).start()

    def clear(part):
        part[...] = jnp.zeros(part.shape, part.dtype)

    barrier = pltpu.get_barrier_semaphore()
    for step in range(1, group):
        pl.semaphore_signal(barrier, inc=1, device_id=(c, g * group + peer(step)), device_id_type=MESH)
    for dt in range(parts):
        for dg in range(groups):
            if (dt, dg) != (0, 0):
                to = ((c + dt) % parts, (g + dg) % groups * group + m)
                pl.semaphore_signal(barrier, inc=1, device_id=to, device_id_type=MESH)

    loads = [
        pltpu.make_async_copy(src, dst, load.at[n])
        for n, (src, dst) in enumerate(
            [
                (const_hbm, const_ref), (pos_t_hbm, pos_t_ref), (pos_w_hbm, pos_w_ref),
                (mask_hbm, mask_in), (q_hbm, q_ref), (pick_hbm, pick_ref),
            ]
        )
    ]
    def row_load(part, kind, p):
        cols = pl.ds(p * heads * dim, dim) if part == 0 else pl.ds((p * heads + 1) * dim, (heads - 1) * dim)
        src, dst = ((k_hbm, k_ref), (v_hbm, v_ref))[kind]
        return pltpu.make_async_copy(src.at[:, :, :, cols], dst.at[:, :, :, cols], kv_load.at[part, kind, p])

    row_loads = [
        [row_load(part, kind, p) for kind in range(2) for p in range(group)] for part in range(2 if heads > 1 else 1)
    ]
    for copy in loads[:4] + row_loads[0] + sum(row_loads[1:], []) + loads[4:]:
        copy.start()

    for copy in loads[:3]:
        copy.wait()

    def column(ref, rows):
        row = ref[...].astype(jnp.float32)
        spread = jnp.broadcast_to(row, (rows, row.shape[1]))
        here = lax.broadcasted_iota(jnp.int32, spread.shape, 0) == lax.broadcasted_iota(jnp.int32, spread.shape, 1)
        return jnp.sum(jnp.where(here, spread, 0.0), axis=1, keepdims=True)

    freq_t = const_ref[width : width + 1, :]
    freq_h = const_ref[width + 1 : width + 2, :]
    freq_w = const_ref[width + 2 : width + 3, :]
    sign = const_ref[width + 3 : width + 4, :]
    pos_h = pos_h_ref[0].astype(jnp.float32)
    angle_hw = pos_h * freq_h + column(pos_w_ref, width) * freq_w
    angle_t = column(pos_t_ref, mask_ref.shape[0]) * freq_t
    for table, of, factor in ((cos_ref, jnp.cos, None), (sin_ref, jnp.sin, sign)):
        of_hw, of_t = of(angle_hw), of(angle_t)
        for f in range(frames):
            part = jnp.where(freq_t > 0, of_t[f : f + 1, :], of_hw)
            table[pl.ds(f * width, width), :] = part if factor is None else part * factor
    for copy in row_loads[0]:
        copy.wait()
    make_rows(0)
    pl.semaphore_wait(barrier, group - 1 + parts * groups - 1)
    send_rows(0)

    pl.when(c == 0)(lambda: clear(ext.at[:, :, 0]))
    pl.when(c == parts - 1)(lambda: clear(ext.at[:, :, frames + 1]))
    pl.when(g == 0)(lambda: clear(ext.at[:, :, :, 0]))
    pl.when(g == groups - 1)(lambda: clear(ext.at[:, :, :, group + 1]))
    clear(mask_pad)

    loads[3].wait()
    slot = mask_ref.shape[1] // mask_in.shape[2]
    for f in range(frames):
        mask_pad[f, pl.ds(0, mask_in.shape[2]), pl.ds(0, mask_in.shape[3])] = (mask_in[f, 0] > 0).astype(jnp.float32)
    clear(mask_ref)
    for f in range(frames):
        tile_rows = mask_pad[f]
        line = tile_rows[0:1, :]
        for b in range(1, mask_in.shape[2]):
            line = line + pltpu.roll(tile_rows, b * slot, 1)[b : b + 1, :]
        mask_ref[f : f + 1, :] = line
    masks[m] = mask_ref[...]

    if heads > 1:
        for copy in row_loads[1]:
            copy.wait()
        make_rows(1)
        rows_left(0)
        send_rows(1)
    for step in range(1, group):
        mask_copy(step).start()

    def spread_on(s):
        for step in range(1, group):
            row_copy(s, step, True).wait_recv()

        @pl.when(c == 0)
        def _():
            for step in range(1, groups):
                first_copy(s, step).start()

        for n in range(len(NEAR)):
            pl.when(near_here(n, 1))(lambda n=n: near_copy(s, n).start())

        def more_rows():
            make_rows(s + 2)
            rows_left(s + 1)
            send_rows(s + 2)

        def more_queries():
            make_queries(s)
            send_queries(s)

        pl.when(s == 0)(loads[4].wait)
        pl.when(s + 2 < heads)(more_rows)
        more_queries()

        @pl.when(c == 0)
        def _():
            first[s, :, pl.ds(g * group, group)] = ext[s, :, 1, pl.ds(1, group)]

    def make_bias():
        for step in range(1, group):
            mask_got(step).wait_recv()
        loads[5].wait()
        for row in range(group):
            spread = jnp.concatenate(
                [jnp.broadcast_to(masks[row, f : f + 1, :], (width, masks.shape[2])) * const_ref[0:width, :] for f in range(frames)],
                axis=0,
            ).astype(jnp.bfloat16)
            allowed = jnp.dot(spread, pick_ref[row], preferred_element_type=jnp.float32)
            allowed = (allowed - 1.0) * 1e30
            bias[:, pl.ds(row * width, width)] = allowed.reshape(frames, width, allowed.shape[1])

    factor = math.log2(math.e) / math.sqrt(dim)

    def pass_on(j):
        for step in range(1, groups):
            first_got(j, step).wait_recv()
        for to in range(1, parts):
            first_on(j, to).start()

    def attend(j):
        pl.when(c > 0)(lambda: first_on(j, 1).wait_recv())
        for n in range(len(NEAR)):
            pl.when(near_here(n, -1))(lambda n=n: near_copy(j, n).wait_recv())

        for step in range(1, group):
            query_copy(j, step, True).wait_recv()
        far_k = first[j, 0].reshape(-1, dim)
        far_v = first[j, 1].reshape(-1, dim)
        far_v = jnp.concatenate([far_v, jnp.ones_like(far_v)], axis=1)
        last = (((1,), (1,)), ((), ()))
        s_all = lax.dot_general(
            q_all[j].reshape(frames * tokens, dim), far_k, last, preferred_element_type=jnp.float32
        )
        near, p_all = [], []
        for f in range(frames):
            q = q_all[j, f].reshape(tokens, dim)
            near_k = ext[j, 0, pl.ds(f, 3)].reshape(-1, dim)
            near_v = ext[j, 1, pl.ds(f, 3)].reshape(-1, dim)
            near_v = jnp.concatenate([near_v, jnp.ones_like(near_v)], axis=1)
            s_near = lax.dot_general(q, near_k, last, preferred_element_type=jnp.float32) + bias[f]
            s_far = s_all[f * tokens : (f + 1) * tokens]
            top = jnp.maximum(
                jnp.max(s_near, axis=1, keepdims=True), jnp.max(s_far, axis=1, keepdims=True)
            )
            p_near = jnp.exp2((s_near - top) * factor).astype(jnp.bfloat16)
            p_all.append(jnp.exp2((s_far - top) * factor).astype(jnp.bfloat16))
            near.append(jnp.dot(p_near, near_v, preferred_element_type=jnp.float32))
        far = jnp.dot(jnp.concatenate(p_all, axis=0), far_v, preferred_element_type=jnp.float32)
        for f in range(frames):
            both = near[f] + far[f * tokens : (f + 1) * tokens]
            result = (both[:, :dim] / both[:, dim:]).astype(jnp.bfloat16)
            held[j, :, pl.ds(f * width, width)] = result.reshape(group, width, dim)
        for step in range(1, group):
            out_copy(j, step).start()
        out_ref[:, columns(m * heads + j)] = held[j, m]

    def turn(s, carry):
        pl.when(s < heads)(lambda: spread_on(s))
        pl.when(s == 0)(make_bias)
        pl.when((c == 0) & (s == heads))(lambda: pass_on(s - 1))
        pl.when(s > 1)(lambda: attend(s - 2))
        pl.when((c == 0) & (s > 0) & (s < heads))(lambda: pass_on(s - 1))
        return carry

    lax.fori_loop(0, heads + 2, turn, 0)

    rows_left(heads - 1)

    def finish(j, carry):
        for step in range(1, group):
            query_copy(j, step, False).wait_send()
            out_copy(j, step).wait_send()
            out_got(j, step).wait_recv()
        for n in range(len(NEAR)):
            pl.when(near_here(n, 1))(lambda n=n: near_copy(j, n).wait_send())

        @pl.when(c == 0)
        def _():
            for step in range(1, groups):
                first_copy(j, step).wait_send()
            for to in range(1, parts):
                first_on(j, to).wait_send()

        return carry

    lax.fori_loop(0, heads, finish, 0)
    for step in range(1, group):
        mask_copy(step).wait_send()


def per_device(parts, high, queries, keys, values, window_mask, pos_t, pos_h, pos_w):
    frames, row_count, width, channels = queries.shape
    assert row_count == 1
    dim = HEAD_DIM
    group = next(n for n in (4, 2, 1) if HEADS % n == 0 and high % n == 0)
    groups, heads = high // group, HEADS // group
    blocks = width // TILE_W
    lanes = 128
    tokens = frames * width
    mask_rows = -(-frames // 8) * 8
    own, pick = mask_selectors(group, width, lanes)
    const = np.concatenate([own, frequencies(dim // 2)], axis=0)
    const = np.pad(const, ((0, -len(const) % 8), (0, 0)))
    keys_near = pick.shape[2]
    sem = pltpu.SemaphoreType.DMA
    in_hbm = functools.partial(pltpu.with_memory_space_constraint, memory_space=pltpu.HBM)
    out = pl.pallas_call(
        functools.partial(kernel, (group, groups, parts, frames, width, heads)),
        out_shape=jax.ShapeDtypeStruct((tokens, channels), jnp.bfloat16),
        in_specs=[pl.BlockSpec(memory_space=pltpu.SMEM if n == 5 else pltpu.HBM) for n in range(9)],
        out_specs=pl.BlockSpec(memory_space=pltpu.VMEM),
        scratch_shapes=[
            pltpu.VMEM(queries.shape, jnp.bfloat16),
            pltpu.VMEM(queries.shape, jnp.bfloat16),
            pltpu.VMEM(queries.shape, jnp.bfloat16),
            pltpu.VMEM(window_mask.shape, jnp.int32),
            pltpu.VMEM((1, frames), jnp.int32),
            pltpu.VMEM((1, width), jnp.int32),
            pltpu.VMEM(const.shape, jnp.float32),
            pltpu.VMEM(pick.shape, jnp.bfloat16),
            pltpu.VMEM((tokens, dim), jnp.float32),
            pltpu.VMEM((tokens, dim), jnp.float32),
            pltpu.VMEM((frames, -(-blocks // 8) * 8, lanes), jnp.float32),
            pltpu.VMEM((mask_rows, lanes), jnp.float32),
            pltpu.VMEM((HEADS, frames, width, dim), jnp.bfloat16),
            pltpu.VMEM((HEADS, 2, frames, width, dim), jnp.bfloat16),
            pltpu.VMEM((heads, frames, group, width, dim), jnp.bfloat16),
            pltpu.VMEM((heads, 2, frames + 2, group + 2, width, dim), jnp.bfloat16),
            pltpu.VMEM((heads, 2, high, width, dim), jnp.bfloat16),
            pltpu.VMEM((heads, group, tokens, dim), jnp.bfloat16),
            pltpu.VMEM((group, mask_rows, lanes), jnp.float32),
            pltpu.VMEM((frames, group * width, keys_near), jnp.float32),
            sem((6,)),
            sem((2, 2, group)),
            sem((heads, max(1, group - 1))),
            sem((heads, group)),
            sem((heads, max(1, group - 1))),
            sem((heads, group)),
            sem((heads, len(NEAR))),
            sem((heads, len(NEAR))),
            sem((heads, max(1, groups - 1))),
            sem((heads, groups)),
            sem((heads, max(1, parts - 1))),
            sem((heads,)),
            sem((heads, max(1, group - 1))),
            sem((heads, group)),
            sem((max(1, group - 1),)),
            sem((group,)),
        ],
        compiler_params=pltpu.CompilerParams(
            collective_id=0, has_side_effects=True, vmem_limit_bytes=48 * 1024 * 1024
        ),
    )(
        *(in_hbm(x) for x in (queries, keys, values, window_mask)),
        in_hbm(pos_t.reshape(1, -1)),
        pos_h,
        in_hbm(pos_w.reshape(1, -1)),
        in_hbm(jnp.asarray(const)),
        in_hbm(jnp.asarray(pick, jnp.bfloat16)),
    )
    return out.reshape(queries.shape)


def solution(mesh):
    return jax.shard_map(
        functools.partial(per_device, mesh.shape["tm"], mesh.shape["height"]),
        mesh=mesh,
        in_specs=(
            P("tm", "height", None, None),
            P("tm", "height", None, None),
            P("tm", "height", None, None),
            P("tm", "height", None, None),
            P("tm"),
            P("height"),
            P(),
        ),
        out_specs=P("tm", "height", None, None),
        check_vma=False,
    )
```
